32 devices in a mesh: dp: 4 (over z), pipe: 4 (over y, x), seq: 2 (over core).
Axes of the slice: x: 2, y: 2, z: 4, core: 2. Of those that a mesh axis runs over, the one named last changes fastest.
Arguments:
- section_input: bfloat16 [4, 4, 256, 1024], P('pipe', 'dp', 'seq'), may hold values from -6 to 6
- event_ids: int32 [4, 256], P('dp', 'seq'), may hold values from 0 to 63
- lengths: int32 [4], P('dp'), may hold values from 64 to 256, as said below
- clicks: int32 [4, 256], P('dp', 'seq'), may hold values 0 or 1
- conversions: int32 [4, 256], P('dp', 'seq'), may hold values 0 or 1
- conv_weight: bfloat16 [4, 3072, 1024], P('pipe'), may hold values from -0.109375 to 0.109375
- type_table: bfloat16 [4, 64, 1024], P('pipe'), may hold values from -3 to 3
- head_weight: bfloat16 [2, 1024], replicated, may hold values from -0.375 to 0.375
Outputs:
- conv_grad: float32 [4, 3072, 1024], P('pipe', ('dp', 'seq'))
- type_grad: float32 [4, 64, 1024], P('pipe', ('dp', 'seq'))
- input_grad: bfloat16 [4, 4, 256, 1024], P('pipe', 'dp', 'seq')
The draws below stay inside these ranges and needn't reach their ends.
Inputs may be any that keep to these rules, and one draw needn't show every extreme that they name: `lengths`: some history has all 256 events real.
All inputs are finite; a program needn't handle non-finite values. No bound on the sum of `clicks` or of `conversions` on one device may be relied on, other than what follows from the above.
Results may differ from the reference program's by a relative error of at most 0.013.
Values may be sent and summed in bfloat16 or wider, within the bound.
A program may use at most 256 MiB of HBM per device.

```python
import math
import jax
import jax.numpy as jnp
import numpy as np
from jax import lax

D = 1024
TYPES = 64
KERNEL = 3
S_DEV = 128
SEQ = 256
LAYERS = 4
USERS = 4
N_PIPE = 4


def draw_lengths(key, part):
    key_len = jax.random.fold_in(key, 11)
    key_pick = jax.random.fold_in(key, 12)
    drawn = SEQ // 4 + jax.random.randint(key_len, (USERS,), 0, SEQ - SEQ // 4 + 1, dtype=jnp.int32)
    chosen = jax.random.randint(key_pick, (), 0, USERS, dtype=jnp.int32)
    return jnp.where(jnp.arange(USERS, dtype=jnp.int32) == chosen, jnp.int32(SEQ), drawn).astype(jnp.int32)


def plant(array, stream_key, low, high):
    spot = [jax.random.randint(jax.random.fold_in(stream_key, axis), (), 0, length) for axis, length in enumerate(array.shape)]
    widest = array.shape.index(max(array.shape))
    next_to = spot[:widest] + [(spot[widest] + 1) % array.shape[widest]] + spot[widest + 1:]
    return array.at[tuple(spot)].set(low).at[tuple(next_to)].set(high)


def block_scale(stream_key, extent, shards, least, high):
    gain, own = 1.0, jax.random.fold_in(stream_key, 6)
    for dim, shards_of in shards:
        draws = jnp.exp(jax.random.uniform(jax.random.fold_in(own, dim), (shards_of,), jnp.float32, least / len(shards), high / len(shards)))
        gain = gain * jnp.repeat(draws, extent[dim] // shards_of).reshape([-1 if axis == dim else 1 for axis in range(len(extent))])
    return gain


def rank_bounds(count, lean):
    loads = [(1 << 20) // math.isqrt(rank ** lean) + 1 for rank in range(1, count + 1)]
    spread = 1 + sum(loads) // (1 << 30)
    return np.cumsum(np.array([max(1, weight // spread) for weight in loads]))


def skewed_ids(own_key, extent, amount, slope):
    grid = rank_bounds(amount, slope)
    pick = jax.random.randint(jax.random.fold_in(own_key, 1), extent, 0, int(grid[amount - 1]))
    rank = jnp.searchsorted(jnp.asarray(grid, jnp.int32), pick, side="right")
    return jax.random.permutation(jax.random.fold_in(own_key, 2), amount)[rank].astype(jnp.int32)


def scatter_about(own_key, shape, scale, bound, split=(), kind=jnp.bfloat16):
    array = jax.random.normal(own_key, shape, jnp.float32) * scale
    if len(split) > 0:
        array = block_scale(own_key, shape, split, -0.22, 0.18) * array
    return jnp.clip(array, min=-bound, max=bound).astype(kind)


def setup_inputs(seed: int = 0) -> dict:
    key_of = jax.random.split(jax.random.key(seed), 9)
    section_input = scatter_about(key_of[0], (N_PIPE, USERS, SEQ, D), 1.0, 6.0, ((0, 4), (1, 4), (2, 2)))
    event_ids = plant(skewed_ids(key_of[1], (USERS, SEQ), TYPES, 2), jax.random.fold_in(key_of[1], 3), 0, TYPES - 1).astype(jnp.int32)
    lengths = draw_lengths(jax.random.fold_in(key_of[8], 71), 0)
    clicks = plant((jax.random.randint(key_of[3], (USERS, SEQ), 0, 3) < 1).astype(jnp.int32), jax.random.fold_in(key_of[3], 1), 0, 1)
    conversions = plant((jax.random.randint(key_of[4], (USERS, SEQ), 0, 2) < 1).astype(jnp.int32), jax.random.fold_in(key_of[4], 1), 0, 1)
    conv_weight = scatter_about(key_of[5], (LAYERS, KERNEL * D, D), (KERNEL * D) ** -0.5, 0.109375, ((0, 4),))
    type_table = scatter_about(key_of[6], (LAYERS, TYPES, D), 0.5, 3.0, ((0, 4),))
    head_weight = scatter_about(key_of[7], (2, D), (D // 4) ** -0.5, 0.375)
    return {"section_input": section_input, "event_ids": event_ids, "lengths": lengths, "clicks": clicks, "conversions": conversions, "conv_weight": conv_weight, "type_table": type_table, "head_weight": head_weight}


EPS = 1e-06

def head_grad(out_bf, head_weight, click, convert, valid):
    logits = jnp.dot(out_bf, head_weight.T, preferred_element_type=jnp.float32)
    label_y = click.astype(jnp.float32)
    label_z = label_y * convert.astype(jnp.float32)
    weight_m = valid.astype(jnp.float32)

    def event_loss(first, second):
        soft = jax.nn.softplus
        rest = jnp.log(jax.nn.sigmoid(-first) + jax.nn.sigmoid(first) * jax.nn.sigmoid(-second))
        return label_y * soft(-first) + (1.0 - label_y) * soft(first) + label_z * (soft(-first) + soft(-second)) - (1.0 - label_z) * rest
    _, pull = jax.vjp(event_loss, logits[:, 0], logits[:, 1])
    grad_first, grad_second = pull(weight_m)
    grad_logits = jnp.stack([grad_first, grad_second], axis=1)
    return jnp.dot(grad_logits, head_weight.astype(jnp.float32), precision=lax.Precision.HIGHEST)

def delayed(values, steps):
    return jnp.concatenate([jnp.zeros((steps, values.shape[1]), values.dtype), values[:values.shape[0] - steps]], axis=0)

def advanced(values, steps):
    return jnp.concatenate([values[steps:], jnp.zeros((steps, values.shape[1]), values.dtype)], axis=0)

def reference(section_input, event_ids, lengths, clicks, conversions, conv_weight, type_table, head_weight):
    conv_list = []
    type_list = []
    grad_list = []
    incoming = None
    for section in reversed(range(LAYERS)):
        spacing = S_DEV // (4 * 2 ** section)
        weight = conv_weight[section]
        table = type_table[section]
        conv_total = jnp.zeros((KERNEL * D, D), jnp.float32)
        type_total = jnp.zeros((TYPES, D), jnp.float32)
        outgoing = []
        for user in range(USERS):
            inputs = section_input[section, user].astype(jnp.float32)
            inv_rms = lax.rsqrt(lax.optimization_barrier(jnp.mean(inputs * inputs, axis=-1, keepdims=True)) + EPS)
            normed = inputs * inv_rms
            normed_bf = normed.astype(jnp.bfloat16)
            taps = jnp.concatenate([delayed(normed_bf, tap * spacing) for tap in range(KERNEL)], axis=1)
            onehot = (event_ids[user][:, None] == jnp.arange(TYPES, dtype=jnp.int32)[None, :]).astype(jnp.bfloat16)
            pre = jnp.dot(taps, weight, preferred_element_type=jnp.float32) + jnp.dot(onehot, table, preferred_element_type=jnp.float32)
            if section == LAYERS - 1:
                out_bf = (inputs + jax.nn.gelu(pre)).astype(jnp.bfloat16)
                valid = jnp.arange(SEQ, dtype=jnp.int32) < lengths[user]
                grad_out = head_grad(out_bf, head_weight, clicks[user], conversions[user], valid)
            else:
                grad_out = incoming[user].astype(jnp.float32)
            _, pull = jax.vjp(jax.nn.gelu, pre)
            grad_pre = pull(grad_out)[0].astype(jnp.bfloat16)
            conv_total = conv_total + lax.dot_general(taps, grad_pre, (((0,), (0,)), ((), ())), preferred_element_type=jnp.float32)
            type_total = type_total + lax.dot_general(onehot, grad_pre, (((0,), (0,)), ((), ())), preferred_element_type=jnp.float32)
            grad_taps = lax.dot_general(grad_pre, weight, (((1,), (1,)), ((), ())), preferred_element_type=jnp.float32)
            grad_normed = grad_taps[:, :D]
            for tap in range(1, KERNEL):
                grad_normed = grad_normed + advanced(grad_taps[:, tap * D:(tap + 1) * D], tap * spacing)
            inner = lax.optimization_barrier(jnp.mean(grad_normed * normed, axis=-1, keepdims=True))
            grad_in = grad_out + inv_rms * (grad_normed - normed * inner)
            outgoing.append(grad_in.astype(jnp.bfloat16))
        incoming = outgoing
        conv_list.append(conv_total)
        type_list.append(type_total)
        grad_list.append(jnp.stack(outgoing, axis=0))
    conv_grad = jnp.stack(conv_list[::-1], axis=0)
    type_grad = jnp.stack(type_list[::-1], axis=0)
    input_grad = jnp.stack(grad_list[::-1], axis=0)
    return (conv_grad, type_grad, input_grad)
```

```python
import jax
import jax.numpy as jnp
from jax import lax
from jax.sharding import PartitionSpec as P

KERNEL = 3


EPS = 1e-06


def from_behind(array, axis, by):
    count = lax.axis_size(axis)
    pairs = [(i, i + by) for i in range(count) if 0 <= i + by < count]
    return lax.ppermute(array, axis, pairs)


def head_grad(out_bf, head_weight, click, convert, valid):
    logits = jnp.dot(out_bf, head_weight.T, preferred_element_type=jnp.float32)
    label_y = click.astype(jnp.float32)
    label_z = label_y * convert.astype(jnp.float32)
    weight_m = valid.astype(jnp.float32)

    def event_loss(first, second):
        soft = jax.nn.softplus
        rest = jnp.log(jax.nn.sigmoid(-first) + jax.nn.sigmoid(first) * jax.nn.sigmoid(-second))
        return (
            label_y * soft(-first)
            + (1.0 - label_y) * soft(first)
            + label_z * (soft(-first) + soft(-second))
            - (1.0 - label_z) * rest
        )

    _, pull = jax.vjp(event_loss, logits[:, 0], logits[:, 1])
    grad_first, grad_second = pull(weight_m)
    heads = head_weight.astype(jnp.float32)
    return grad_first[:, None] * heads[0][None] + grad_second[:, None] * heads[1][None]


def on_device(
    section_input, event_ids, lengths, clicks, conversions, conv_weight, type_table, head_weight
):
    inputs_bf = section_input[0, 0]
    rows, width = inputs_bf.shape
    halo_rows = rows // 2
    weight = conv_weight[0]
    table = type_table[0]
    kinds = table.shape[0]
    section = lax.axis_index("pipe")
    sections = lax.axis_size("pipe")
    users, shards = lax.axis_size("dp"), lax.axis_size("seq")
    spacing = jnp.right_shift(jnp.int32(rows // 4), section)
    inputs = inputs_bf.astype(jnp.float32)
    inv_rms = lax.rsqrt(jnp.mean(inputs * inputs, axis=-1, keepdims=True) + EPS)
    normed = inputs * inv_rms
    normed_bf = normed.astype(jnp.bfloat16)
    earlier = from_behind(normed_bf[rows - halo_rows :], "seq", 1)
    normed_all = lax.all_gather(normed_bf, ("dp", "seq"), axis=0, tiled=True)
    ids_all = lax.all_gather(event_ids[0], ("dp", "seq"), axis=0, tiled=True)
    extended = jnp.concatenate([earlier, normed_bf], axis=0)
    onehot = (event_ids[0][:, None] == jnp.arange(kinds, dtype=jnp.int32)[None, :]).astype(
        jnp.bfloat16
    )
    position = lax.axis_index("seq") * rows + jnp.arange(rows, dtype=jnp.int32)
    valid = position < lengths[0]
    is_last = section == sections - 1

    pre = jnp.dot(onehot, table, preferred_element_type=jnp.float32)
    for tap in range(KERNEL):
        shifted = lax.dynamic_slice_in_dim(extended, halo_rows - tap * spacing, rows, 0)
        pre = pre + jnp.dot(
            shifted, weight[tap * width : (tap + 1) * width], preferred_element_type=jnp.float32
        )
    active, pull = jax.vjp(jax.nn.gelu, pre)
    slope = pull(jnp.ones_like(pre))[0]
    out_bf = (inputs + active).astype(jnp.bfloat16)
    top_grad = head_grad(out_bf, head_weight, clicks[0], conversions[0], valid)

    incoming = jnp.zeros((rows, width), jnp.bfloat16)
    for tick in range(sections):
        grad_out = jnp.where(is_last, top_grad, incoming.astype(jnp.float32))
        grad_pre = (grad_out * slope).astype(jnp.bfloat16)
        later = from_behind(grad_pre[:halo_rows], "seq", -1)
        grad_ext = jnp.concatenate([grad_pre, later], axis=0)
        grad_normed = jnp.zeros((rows, width), jnp.float32)
        for tap in range(KERNEL):
            shifted = lax.dynamic_slice_in_dim(grad_ext, tap * spacing, rows, 0)
            grad_normed = grad_normed + lax.dot_general(
                shifted,
                weight[tap * width : (tap + 1) * width],
                (((1,), (1,)), ((), ())),
                preferred_element_type=jnp.float32,
            )
        inner = jnp.mean(grad_normed * normed, axis=-1, keepdims=True)
        grad_in = (grad_out + inv_rms * (grad_normed - normed * inner)).astype(jnp.bfloat16)
        if tick + 1 < sections:
            incoming = from_behind(grad_in, "pipe", -1)

    grad_all = lax.all_gather(grad_pre, ("dp", "seq"), axis=0, tiled=True)
    owner = lax.axis_index("dp") * shards + lax.axis_index("seq")
    share = KERNEL * width // (users * shards)
    start = owner * share
    wide = jnp.concatenate([normed_all, normed_all], axis=1)
    mine = lax.dynamic_slice_in_dim(wide, lax.rem(start, width), share, 1)
    mine = mine.reshape(users, shards * rows, share)
    tap_of = lax.div(start + jnp.arange(share, dtype=jnp.int32), width)
    padded = jnp.pad(mine, ((0, 0), (2 * halo_rows, 0), (0, 0)))
    part = mine
    for tap in range(1, KERNEL):
        moved = lax.dynamic_slice_in_dim(
            padded, 2 * halo_rows - tap * spacing, shards * rows, 1
        )
        part = jnp.where((tap_of == tap)[None, None, :], moved, part)
    part = part.reshape(users * shards * rows, share)
    conv_share = lax.dot_general(
        part, grad_all, (((0,), (0,)), ((), ())), preferred_element_type=jnp.float32
    )
    kind_share = kinds // (users * shards)
    kind = owner * kind_share + jnp.arange(kind_share, dtype=jnp.int32)
    picks = (ids_all[:, None] == kind[None, :]).astype(jnp.bfloat16)
    type_share = lax.dot_general(
        picks, grad_all, (((0,), (0,)), ((), ())), preferred_element_type=jnp.float32
    )
    return (conv_share[None], type_share[None], grad_in[None, None])


def solution(mesh):
    placed = (
        P("pipe", "dp", "seq", None),
        P("dp", "seq"),
        P("dp"),
        P("dp", "seq"),
        P("dp", "seq"),
        P("pipe", None, None),
        P("pipe", None, None),
        P(),
    )
    return jax.shard_map(
        on_device,
        mesh=mesh,
        in_specs=placed,
        out_specs=(
            P("pipe", ("dp", "seq"), None),
            P("pipe", ("dp", "seq"), None),
            P("pipe", "dp", "seq", None),
        ),
        check_vma=False,
    )
```

```python
import functools

import jax
import jax.numpy as jnp
from jax import lax
from jax.experimental import pallas as pl
from jax.experimental.pallas import tpu as pltpu
from jax.sharding import PartitionSpec as P

KERNEL = 3
EPS = 1e-06
BLOCK = 256
MESH = pl.DeviceIdType.MESH


def kernel(
    users, shards, sections, kind_share,
    x_ref, row_ref, weight_hbm, table_ref, head_ref,
    conv_ref, type_ref, gin_ref,
    weight_ref, ext, taps, back, tap_src, tap_all, slope, gnorm, gout, gp_all, halo_out, halo_in,
    back_in, inc, gin_buf,
    w_sem, halo_sem, back_sem, pipe_sem, tap_send, tap_recv, dp_send, dp_recv, f_send, f_recv,
):
    rows, width = x_ref.shape
    half = rows // 2
    dp, section, seq = lax.axis_index("dp"), lax.axis_index("pipe"), lax.axis_index("seq")
    group = users * shards
    me = dp * shards + seq
    share = KERNEL * width // group
    is_last = section == sections - 1
    f32, bf16 = jnp.float32, jnp.bfloat16

    for tap in range(KERNEL):
        part = pl.ds(tap * width, width)
        pltpu.make_async_copy(weight_hbm.at[part], weight_ref.at[part], w_sem.at[tap]).start()

    barrier = pltpu.get_barrier_semaphore()

    def peer_id(i):
        peer = lax.rem(me + i, group)
        return peer, lax.div(peer, shards), lax.rem(peer, shards)

    @pl.loop(1, group)
    def _(i):
        _, d, s = peer_id(i)
        pl.semaphore_signal(barrier, inc=1, device_id={"dp": d, "seq": s}, device_id_type=MESH)

    @pl.when(section > 0)
    def _():
        pl.semaphore_signal(barrier, inc=1, device_id={"pipe": section - 1}, device_id_type=MESH)

    @pl.when(section < sections - 1)
    def _():
        pl.semaphore_signal(barrier, inc=1, device_id={"pipe": section + 1}, device_id_type=MESH)

    x = x_ref[...].astype(f32)
    inv = lax.rsqrt(jnp.mean(x * x, axis=-1, keepdims=True) + EPS)
    normed = x * inv
    normed_bf = normed.astype(bf16)
    halo_out[...] = normed_bf[half:]

    pipe_peers = (section > 0).astype(jnp.int32) + (section < sections - 1).astype(jnp.int32)
    pl.semaphore_wait(barrier, group - 1 + pipe_peers)

    def halo_copy(to):
        return pltpu.make_async_remote_copy(
            src_ref=halo_out, dst_ref=halo_in, send_sem=halo_sem.at[0], recv_sem=halo_sem.at[1],
            device_id={"seq": to}, device_id_type=MESH,
        )

    @pl.when(seq < shards - 1)
    def _():
        halo_copy(seq + 1).start()

    ext[half:] = normed_bf.astype(f32)
    taps[0] = normed_bf

    @pl.when(seq == 0)
    def _():
        ext[:half] = jnp.zeros((half, width), f32)

    @pl.when(seq > 0)
    def _():
        halo_copy(seq - 1).wait_recv()
        ext[:half] = halo_in[...].astype(f32)

    def shifted(dest, slot, base, way, tap):
        for place in range(sections):
            start = base + way * tap * (rows // 4 >> place)

            @pl.when(section == place)
            def _():
                dest[slot] = ext[start : start + rows].astype(bf16)

    for tap in range(1, KERNEL):
        shifted(taps, tap, half, -1, tap)
    for tap in range(KERNEL):
        part = pl.ds(tap * width, width)
        pltpu.make_async_copy(weight_hbm.at[part], weight_ref.at[part], w_sem.at[tap]).wait()

    info = row_ref[...]
    kinds = table_ref.shape[0]
    ids = jnp.broadcast_to(info[3:4], (kinds, rows)).astype(jnp.int32)
    pick = jnp.where(ids == lax.broadcasted_iota(jnp.int32, (kinds, rows), 0), 1.0, 0.0).astype(f32)
    onehot = jnp.transpose(pick).astype(bf16)

    def forward(i, logits):
        cols = pl.ds(pl.multiple_of(i * BLOCK, BLOCK), BLOCK)
        pre = jnp.dot(onehot, table_ref[:, cols], preferred_element_type=f32)
        for tap in range(KERNEL):
            pre = pre + jnp.dot(
                taps[tap], weight_ref[tap * width : (tap + 1) * width, cols],
                preferred_element_type=f32,
            )
        square = pre * pre
        scale = 0.7978845608028654
        curve = jnp.tanh(scale * (pre + 0.044715 * (square * pre)))
        slope[:, cols] = 0.5 * (1.0 + curve) + 0.5 * pre * (1.0 - curve * curve) * (
            scale * (1.0 + 0.134145 * square)
        )
        out_bf = (x_ref[:, cols].astype(f32) + 0.5 * pre * (1.0 + curve)).astype(bf16)
        return logits + lax.dot_general(
            head_ref[:, cols], out_bf, (((1,), (1,)), ((), ())), preferred_element_type=f32
        )

    logits = lax.fori_loop(0, width // BLOCK, forward, jnp.zeros((8, rows), f32))

    def send_taps():
        block_rows = tap_src.shape[1]
        for tap in range(KERNEL):
            weight_rows = jnp.transpose(taps[tap].astype(f32)).astype(bf16)
            low = tap * width
            while low < (tap + 1) * width:
                peer = low // share
                high = min((peer + 1) * share, (tap + 1) * width)
                tap_src[peer, low - peer * share : high - peer * share] = weight_rows[
                    low - tap * width : high - tap * width
                ]
                low = high
        ids_rows = jnp.broadcast_to(row_ref[3:4], (block_rows - share, rows)).astype(bf16)
        for peer in range(group):
            tap_src[peer, share:] = ids_rows

        @pl.loop(1, group)
        def _(i):
            peer, d, s = peer_id(i)
            pltpu.make_async_remote_copy(
                src_ref=tap_src.at[peer],
                dst_ref=tap_all.at[me],
                send_sem=tap_send.at[peer], recv_sem=tap_recv.at[me],
                device_id={"dp": d, "seq": s}, device_id_type=MESH,
            ).start()
        tap_all[me] = tap_src[me]

    def pipe_copy(to):
        return pltpu.make_async_remote_copy(
            src_ref=gin_buf, dst_ref=inc, send_sem=pipe_sem.at[0], recv_sem=pipe_sem.at[1],
            device_id={"pipe": to}, device_id_type=MESH,
        )

    @pl.when(is_last)
    def _():
        a, b = logits[0:1], logits[1:2]
        y, z, m = info[0:1], info[1:2], info[2:3]
        sa, na = jax.nn.sigmoid(a), jax.nn.sigmoid(-a)
        sb, nb = jax.nn.sigmoid(b), jax.nn.sigmoid(-b)
        rest = (1.0 - z) / (na + sa * nb)
        first = m * ((1.0 - y) * sa - (y + z) * na + rest * (sa * na * sb))
        second = m * (rest * (sa * sb * nb) - z * nb)
        columns = jnp.transpose(
            jnp.concatenate([first, second, jnp.zeros((6, rows), f32)], axis=0)
        )
        heads = head_ref[...].astype(f32)
        gout[...] = columns[:, 0:1] * heads[0:1] + columns[:, 1:2] * heads[1:2]

    @pl.when(section < sections - 1)
    def _():
        send_taps()
        pipe_copy(section + 1).wait_recv()
        gout[...] = inc[...].astype(f32)

    mine = pl.ds(pl.multiple_of(me * rows, rows), rows)
    grad_pre = (gout[...] * slope[...]).astype(bf16)
    gp_all[mine] = grad_pre

    def back_copy(to):
        return pltpu.make_async_remote_copy(
            src_ref=gp_all.at[pl.ds(pl.multiple_of(me * rows, rows), half)], dst_ref=back_in,
            send_sem=back_sem.at[0], recv_sem=back_sem.at[1],
            device_id={"seq": to}, device_id_type=MESH,
        )

    @pl.when(seq > 0)
    def _():
        back_copy(seq - 1).start()

    def dp_copy(source, to):
        piece = gp_all.at[pl.ds(pl.multiple_of((source * shards + seq) * rows, rows), rows)]
        return pltpu.make_async_remote_copy(
            src_ref=piece, dst_ref=piece, send_sem=dp_send.at[to], recv_sem=dp_recv.at[source],
            device_id={"dp": to}, device_id_type=MESH,
        )

    def seq_copy(user, source, to):
        piece = gp_all.at[pl.ds(pl.multiple_of((user * shards + source) * rows, rows), rows)]
        return pltpu.make_async_remote_copy(
            src_ref=piece, dst_ref=piece, send_sem=f_send.at[user, to],
            recv_sem=f_recv.at[user, source], device_id={"seq": to}, device_id_type=MESH,
        )

    @pl.loop(1, users)
    def _(i):
        dp_copy(dp, lax.rem(dp + i, users)).start()

    def times(lhs, tap, first):
        @pl.loop(0, width // BLOCK)
        def _(i):
            cols = pl.ds(pl.multiple_of(i * BLOCK, BLOCK), BLOCK)
            rows_of = pl.ds(pl.multiple_of(tap * width + i * BLOCK, BLOCK), BLOCK)
            value = lax.dot_general(
                lhs[...], weight_ref[rows_of], (((1,), (1,)), ((), ())),
                preferred_element_type=f32,
            )
            gnorm[:, cols] = value if first else gnorm[:, cols] + value

    times(gp_all.at[mine], 0, True)
    ext[:rows] = grad_pre.astype(f32)

    @pl.when(seq == shards - 1)
    def _():
        ext[rows:] = jnp.zeros((half, width), f32)

    @pl.when(seq < shards - 1)
    def _():
        back_copy(seq + 1).wait_recv()
        ext[rows:] = back_in[...].astype(f32)

    for tap in range(1, KERNEL):
        shifted(back, tap - 1, 0, 1, tap)
        times(back.at[tap - 1], tap, False)
    x = x_ref[...].astype(f32)
    inv = lax.rsqrt(jnp.mean(x * x, axis=-1, keepdims=True) + EPS)
    normed = x * inv
    grad_normed = gnorm[...]
    inner = jnp.mean(grad_normed * normed, axis=-1, keepdims=True)
    gin_buf[...] = (gout[...] + inv * (grad_normed - normed * inner)).astype(bf16)

    @pl.when(section > 0)
    def _():
        pipe_copy(section - 1).start()

    gin_ref[...] = gin_buf[...]

    @pl.when(is_last)
    def _():
        send_taps()

    @pl.loop(1, shards)
    def _(i):
        seq_copy(dp, seq, lax.rem(seq + i, shards)).start()

    @pl.loop(1, users)
    def _(i):
        user = lax.rem(dp + i, users)
        dp_copy(user, user).wait_recv()

        @pl.loop(1, shards)
        def _(j):
            seq_copy(user, seq, lax.rem(seq + j, shards)).start()

    @pl.loop(1, group)
    def _(i):
        peer, d, s = peer_id(i)
        pltpu.make_async_remote_copy(
            src_ref=tap_src.at[peer],
            dst_ref=tap_all.at[peer],
            send_sem=tap_send.at[peer], recv_sem=tap_recv.at[peer],
            device_id={"dp": d, "seq": s}, device_id_type=MESH,
        ).wait()

    @pl.loop(0, users)
    def _(user):
        @pl.loop(1, shards)
        def _(j):
            seq_copy(user, lax.rem(seq + j, shards), lax.rem(seq + j, shards)).wait()

    kind = me * kind_share + lax.broadcasted_iota(
        jnp.int32, (tap_src.shape[1] - share, rows), 0
    )
    conv_ref[...] = jnp.zeros_like(conv_ref)
    type_ref[...] = jnp.zeros_like(type_ref)

    @pl.loop(0, users)
    def _(user):
        pieces = [tap_all[user * shards + s] for s in range(shards)]
        left = jnp.concatenate([piece[:share] for piece in pieces], axis=1)
        picks = jnp.concatenate(
            [
                jnp.where(piece[share:].astype(f32).astype(jnp.int32) == kind, 1.0, 0.0).astype(bf16)
                for piece in pieces
            ],
            axis=1,
        )
        span = pl.ds(pl.multiple_of(user * shards * rows, shards * rows), shards * rows)
        for i in range(width // BLOCK):
            cols = slice(i * BLOCK, (i + 1) * BLOCK)
            right = gp_all[span, cols]
            conv_ref[:, cols] += jnp.dot(left, right, preferred_element_type=f32)
            type_ref[:, cols] += jnp.dot(picks, right, preferred_element_type=f32)[:kind_share]

    @pl.loop(1, users)
    def _(i):
        dp_copy(dp, lax.rem(dp + i, users)).wait_send()

    @pl.when(section > 0)
    def _():
        pipe_copy(section - 1).wait_send()

    @pl.when(seq > 0)
    def _():
        back_copy(seq - 1).wait_send()

    @pl.when(seq < shards - 1)
    def _():
        halo_copy(seq + 1).wait_send()


def on_device(
    section_input, event_ids, lengths, clicks, conversions, conv_weight, type_table, head_weight
):
    inputs_bf = section_input[0, 0]
    rows, width = inputs_bf.shape
    half = rows // 2
    kinds = type_table.shape[1]
    users, shards, sections = (lax.axis_size(name) for name in ("dp", "seq", "pipe"))
    group = users * shards
    share = KERNEL * width // group
    kind_share = kinds // group
    block_rows = share + -(-kind_share // 16) * 16
    position = lax.axis_index("seq") * rows + jnp.arange(rows, dtype=jnp.int32)
    label = clicks[0].astype(jnp.float32)
    lines = jnp.stack(
        [
            label,
            label * conversions[0].astype(jnp.float32),
            (position < lengths[0]).astype(jnp.float32),
            event_ids[0].astype(jnp.float32),
        ]
    )
    lines = jnp.pad(lines, ((0, 4), (0, 0)))
    heads = jnp.pad(head_weight, ((0, 6), (0, 0)))
    vmem = pl.BlockSpec(memory_space=pltpu.VMEM)
    dma = pltpu.SemaphoreType.DMA
    f32, bf16 = jnp.float32, jnp.bfloat16
    conv, kind, grad_in = pl.pallas_call(
        functools.partial(kernel, users, shards, sections, kind_share),
        out_shape=(
            jax.ShapeDtypeStruct((share, width), f32),
            jax.ShapeDtypeStruct((kind_share, width), f32),
            jax.ShapeDtypeStruct((rows, width), bf16),
        ),
        in_specs=[vmem, vmem, pl.BlockSpec(memory_space=pl.ANY), vmem, vmem],
        out_specs=(vmem, vmem, vmem),
        scratch_shapes=[
            pltpu.VMEM((KERNEL * width, width), bf16),
            pltpu.VMEM((rows + half, width), f32),
            pltpu.VMEM((KERNEL, rows, width), bf16),
            pltpu.VMEM((KERNEL - 1, rows, width), bf16),
            pltpu.VMEM((group, block_rows, rows), bf16),
            pltpu.VMEM((group, block_rows, rows), bf16),
            pltpu.VMEM((rows, width), f32),
            pltpu.VMEM((rows, width), f32),
            pltpu.VMEM((rows, width), f32),
            pltpu.VMEM((group * rows, width), bf16),
            pltpu.VMEM((half, width), bf16),
            pltpu.VMEM((half, width), bf16),
            pltpu.VMEM((half, width), bf16),
            pltpu.VMEM((rows, width), bf16),
            pltpu.VMEM((rows, width), bf16),
            dma((KERNEL,)),
            dma((2,)),
            dma((2,)),
            dma((2,)),
            dma((group,)),
            dma((group,)),
            dma((users,)),
            dma((users,)),
            dma((users, shards)),
            dma((users, shards)),
        ],
        compiler_params=pltpu.CompilerParams(
            collective_id=0, has_side_effects=True, vmem_limit_bytes=56 * 1024 * 1024
        ),
    )(inputs_bf, lines, conv_weight[0], type_table[0], heads)
    return (conv[None], kind[None], grad_in[None, None])


def solution(mesh):
    placed = (
        P("pipe", "dp", "seq", None),
        P("dp", "seq"),
        P("dp"),
        P("dp", "seq"),
        P("dp", "seq"),
        P("pipe", None, None),
        P("pipe", None, None),
        P(),
    )
    return jax.shard_map(
        on_device,
        mesh=mesh,
        in_specs=placed,
        out_specs=(
            P("pipe", ("dp", "seq"), None),
            P("pipe", ("dp", "seq"), None),
            P("pipe", "dp", "seq", None),
        ),
        check_vma=False,
    )
```

```python
import functools

import jax
import jax.numpy as jnp
from jax import lax
from jax.experimental import pallas as pl
from jax.experimental.pallas import tpu as pltpu
from jax.sharding import PartitionSpec as P

KERNEL = 3
EPS = 1e-06
BLOCK = 256
MESH = pl.DeviceIdType.MESH


def kernel(
    users, shards, sections, kind_share,
    x_ref, id_ref, click_ref, convert_ref, length_ref, weight_hbm, table_ref, head_ref,
    conv_ref, type_ref, gin_ref,
    weight_ref, ext, taps, back, tap_src, tap_all, slope, gnorm, gout, gp_all, halo_out, halo_in,
    back_in, inc, gin_buf, heads,
    w_sem, halo_sem, back_sem, pipe_sem, tap_send, tap_recv, dp_send, dp_recv, f_send, f_recv,
):
    rows, width = x_ref.shape
    half = rows // 2
    dp, section, seq = lax.axis_index("dp"), lax.axis_index("pipe"), lax.axis_index("seq")
    group = users * shards
    me = dp * shards + seq
    share = KERNEL * width // group
    is_last = section == sections - 1
    f32, bf16 = jnp.float32, jnp.bfloat16

    for tap in range(KERNEL):
        part = pl.ds(tap * width, width)
        pltpu.make_async_copy(weight_hbm.at[part], weight_ref.at[part], w_sem.at[tap]).start()

    barrier = pltpu.get_barrier_semaphore()

    def peer_id(i):
        peer = lax.rem(me + i, group)
        return peer, lax.div(peer, shards), lax.rem(peer, shards)

    @pl.loop(1, group)
    def _(i):
        _, d, s = peer_id(i)
        pl.semaphore_signal(barrier, inc=1, device_id={"dp": d, "seq": s}, device_id_type=MESH)

    @pl.when(section > 0)
    def _():
        pl.semaphore_signal(barrier, inc=1, device_id={"pipe": section - 1}, device_id_type=MESH)

    @pl.when(section < sections - 1)
    def _():
        pl.semaphore_signal(barrier, inc=1, device_id={"pipe": section + 1}, device_id_type=MESH)

    x = x_ref[...].astype(f32)
    inv = lax.rsqrt(jnp.mean(x * x, axis=-1, keepdims=True) + EPS)
    normed = x * inv
    normed_bf = normed.astype(bf16)
    halo_out[...] = normed_bf[half:]

    pipe_peers = (section > 0).astype(jnp.int32) + (section < sections - 1).astype(jnp.int32)
    pl.semaphore_wait(barrier, group - 1 + pipe_peers)

    def halo_copy(to):
        return pltpu.make_async_remote_copy(
            src_ref=halo_out, dst_ref=halo_in, send_sem=halo_sem.at[0], recv_sem=halo_sem.at[1],
            device_id={"seq": to}, device_id_type=MESH,
        )

    @pl.when(seq < shards - 1)
    def _():
        halo_copy(seq + 1).start()

    ext[half:] = normed_bf.astype(f32)
    taps[0] = normed_bf

    @pl.when(seq == 0)
    def _():
        ext[:half] = jnp.zeros((half, width), f32)

    @pl.when(seq > 0)
    def _():
        halo_copy(seq - 1).wait_recv()
        ext[:half] = halo_in[...].astype(f32)

    def shifted(dest, slot, base, way, tap):
        for place in range(sections):
            start = base + way * tap * (rows // 4 >> place)

            @pl.when(section == place)
            def _():
                dest[slot] = ext[start : start + rows].astype(bf16)

    for tap in range(1, KERNEL):
        shifted(taps, tap, half, -1, tap)
    for tap in range(KERNEL):
        part = pl.ds(tap * width, width)
        pltpu.make_async_copy(weight_hbm.at[part], weight_ref.at[part], w_sem.at[tap]).wait()

    id_row = id_ref[...]
    heads[...] = jnp.concatenate(
        [head_ref[...].astype(f32), jnp.zeros((6, width), f32)], axis=0
    )
    kinds = table_ref.shape[0]
    ids = jnp.broadcast_to(id_row, (kinds, rows))
    pick = jnp.where(ids == lax.broadcasted_iota(jnp.int32, (kinds, rows), 0), 1.0, 0.0).astype(f32)
    onehot = jnp.transpose(pick).astype(bf16)

    def forward(i, logits):
        cols = pl.ds(pl.multiple_of(i * BLOCK, BLOCK), BLOCK)
        pre = jnp.dot(onehot, table_ref[:, cols], preferred_element_type=f32)
        for tap in range(KERNEL):
            pre = pre + jnp.dot(
                taps[tap], weight_ref[tap * width : (tap + 1) * width, cols],
                preferred_element_type=f32,
            )
        square = pre * pre
        scale = 0.7978845608028654
        curve = jnp.tanh(scale * (pre + 0.044715 * (square * pre)))
        slope[:, cols] = 0.5 * (1.0 + curve) + 0.5 * pre * (1.0 - curve * curve) * (
            scale * (1.0 + 0.134145 * square)
        )
        out_bf = (x_ref[:, cols].astype(f32) + 0.5 * pre * (1.0 + curve)).astype(bf16)
        return logits + lax.dot_general(
            heads[:, cols].astype(bf16), out_bf, (((1,), (1,)), ((), ())), preferred_element_type=f32
        )

    logits = lax.fori_loop(0, width // BLOCK, forward, jnp.zeros((8, rows), f32))

    def send_taps():
        block_rows = tap_src.shape[1]
        for tap in range(KERNEL):
            weight_rows = jnp.transpose(taps[tap].astype(f32)).astype(bf16)
            low = tap * width
            while low < (tap + 1) * width:
                peer = low // share
                high = min((peer + 1) * share, (tap + 1) * width)
                tap_src[peer, low - peer * share : high - peer * share] = weight_rows[
                    low - tap * width : high - tap * width
                ]
                low = high
        ids_rows = jnp.broadcast_to(id_row.astype(f32), (block_rows - share, rows)).astype(bf16)
        for peer in range(group):
            tap_src[peer, share:] = ids_rows

        @pl.loop(1, group)
        def _(i):
            peer, d, s = peer_id(i)
            pltpu.make_async_remote_copy(
                src_ref=tap_src.at[peer],
                dst_ref=tap_all.at[me],
                send_sem=tap_send.at[peer], recv_sem=tap_recv.at[me],
                device_id={"dp": d, "seq": s}, device_id_type=MESH,
            ).start()
        tap_all[me] = tap_src[me]

    def pipe_copy(to):
        return pltpu.make_async_remote_copy(
            src_ref=gin_buf, dst_ref=inc, send_sem=pipe_sem.at[0], recv_sem=pipe_sem.at[1],
            device_id={"pipe": to}, device_id_type=MESH,
        )

    @pl.when(is_last)
    def _():
        a, b = logits[0:1], logits[1:2]
        y = click_ref[...].astype(f32)
        z = y * convert_ref[...].astype(f32)
        position = seq * rows + lax.broadcasted_iota(jnp.int32, (1, rows), 1)
        m = jnp.where(position < length_ref[0], 1.0, 0.0).astype(f32)
        sa, na = jax.nn.sigmoid(a), jax.nn.sigmoid(-a)
        sb, nb = jax.nn.sigmoid(b), jax.nn.sigmoid(-b)
        rest = (1.0 - z) / (na + sa * nb)
        first = m * ((1.0 - y) * sa - (y + z) * na + rest * (sa * na * sb))
        second = m * (rest * (sa * sb * nb) - z * nb)
        columns = jnp.transpose(
            jnp.concatenate([first, second, jnp.zeros((6, rows), f32)], axis=0)
        )
        gout[...] = columns[:, 0:1] * heads[0:1] + columns[:, 1:2] * heads[1:2]

    @pl.when(section < sections - 1)
    def _():
        send_taps()
        pipe_copy(section + 1).wait_recv()
        gout[...] = inc[...].astype(f32)

    mine = pl.ds(pl.multiple_of(me * rows, rows), rows)
    grad_pre = (gout[...] * slope[...]).astype(bf16)
    gp_all[mine] = grad_pre

    def back_copy(to):
        return pltpu.make_async_remote_copy(
            src_ref=gp_all.at[pl.ds(pl.multiple_of(me * rows, rows), half)], dst_ref=back_in,
            send_sem=back_sem.at[0], recv_sem=back_sem.at[1],
            device_id={"seq": to}, device_id_type=MESH,
        )

    @pl.when(seq > 0)
    def _():
        back_copy(seq - 1).start()

    def line_copy(source, to, way):
        piece = gp_all.at[pl.ds(pl.multiple_of((source * shards + seq) * rows, rows), rows)]
        return pltpu.make_async_remote_copy(
            src_ref=piece, dst_ref=piece, send_sem=dp_send.at[source, way],
            recv_sem=dp_recv.at[source], device_id={"dp": to}, device_id_type=MESH,
        )

    def pass_on(source, left, right):
        if left:

            @pl.when(dp > 0)
            def _():
                line_copy(source, dp - 1, 0).start()

        if right:

            @pl.when(dp < users - 1)
            def _():
                line_copy(source, dp + 1, 1).start()

    def seq_copy(user, source, to):
        piece = gp_all.at[pl.ds(pl.multiple_of((user * shards + source) * rows, rows), rows)]
        return pltpu.make_async_remote_copy(
            src_ref=piece, dst_ref=piece, send_sem=f_send.at[user, to],
            recv_sem=f_recv.at[user, source], device_id={"seq": to}, device_id_type=MESH,
        )

    pass_on(dp, True, True)

    def times(lhs, tap, first):
        @pl.loop(0, width // BLOCK)
        def _(i):
            cols = pl.ds(pl.multiple_of(i * BLOCK, BLOCK), BLOCK)
            rows_of = pl.ds(pl.multiple_of(tap * width + i * BLOCK, BLOCK), BLOCK)
            value = lax.dot_general(
                lhs[...], weight_ref[rows_of], (((1,), (1,)), ((), ())),
                preferred_element_type=f32,
            )
            gnorm[:, cols] = value if first else gnorm[:, cols] + value

    times(gp_all.at[mine], 0, True)
    ext[:rows] = grad_pre.astype(f32)

    @pl.when(seq == shards - 1)
    def _():
        ext[rows:] = jnp.zeros((half, width), f32)

    @pl.when(seq < shards - 1)
    def _():
        back_copy(seq + 1).wait_recv()
        ext[rows:] = back_in[...].astype(f32)

    for tap in range(1, KERNEL):
        shifted(back, tap - 1, 0, 1, tap)
        times(back.at[tap - 1], tap, False)
    x = x_ref[...].astype(f32)
    inv = lax.rsqrt(jnp.mean(x * x, axis=-1, keepdims=True) + EPS)
    normed = x * inv
    grad_normed = gnorm[...]
    inner = jnp.mean(grad_normed * normed, axis=-1, keepdims=True)
    gin_buf[...] = (gout[...] + inv * (grad_normed - normed * inner)).astype(bf16)

    @pl.when(section > 0)
    def _():
        pipe_copy(section - 1).start()

    gin_ref[...] = gin_buf[...]

    @pl.when(is_last)
    def _():
        send_taps()

    def share_out(user):
        @pl.loop(1, shards)
        def _(j):
            seq_copy(user, seq, lax.rem(seq + j, shards)).start()

    share_out(dp)
    conv_ref[...] = jnp.zeros_like(conv_ref)
    type_ref[...] = jnp.zeros_like(type_ref)

    @pl.loop(1, group)
    def _(i):
        peer, d, s = peer_id(i)
        pltpu.make_async_remote_copy(
            src_ref=tap_src.at[peer],
            dst_ref=tap_all.at[peer],
            send_sem=tap_send.at[peer], recv_sem=tap_recv.at[peer],
            device_id={"dp": d, "seq": s}, device_id_type=MESH,
        ).wait()

    kind = me * kind_share + lax.broadcasted_iota(
        jnp.int32, (tap_src.shape[1] - share, rows), 0
    )

    def multiply(user):
        @pl.loop(1, shards)
        def _(j):
            other = lax.rem(seq + j, shards)
            seq_copy(user, other, other).wait()

        pieces = [tap_all[user * shards + s] for s in range(shards)]
        left = jnp.concatenate([piece[:share] for piece in pieces], axis=1)
        picks = jnp.concatenate(
            [
                jnp.where(piece[share:].astype(f32).astype(jnp.int32) == kind, 1.0, 0.0).astype(bf16)
                for piece in pieces
            ],
            axis=1,
        )
        span = pl.ds(pl.multiple_of(user * shards * rows, shards * rows), shards * rows)
        for i in range(width // BLOCK):
            cols = slice(i * BLOCK, (i + 1) * BLOCK)
            right = gp_all[span, cols]
            conv_ref[:, cols] += jnp.dot(left, right, preferred_element_type=f32)
            type_ref[:, cols] += jnp.dot(picks, right, preferred_element_type=f32)[:kind_share]

    @pl.loop(0, users)
    def _(h):
        before, after = dp - h - 1, dp + h + 1

        @pl.when(before >= 0)
        def _():
            line_copy(before, before, 1).wait_recv()
            pass_on(before, False, True)
            share_out(before)

        @pl.when(after < users)
        def _():
            line_copy(after, after, 0).wait_recv()
            pass_on(after, True, False)
            share_out(after)

        @pl.when(dp - h >= 0)
        def _():
            multiply(dp - h)

        @pl.when((h > 0) & (dp + h < users))
        def _():
            multiply(dp + h)

    @pl.loop(0, users)
    def _(source):
        @pl.when((source >= dp) & (dp > 0))
        def _():
            line_copy(source, dp - 1, 0).wait_send()

        @pl.when((source <= dp) & (dp < users - 1))
        def _():
            line_copy(source, dp + 1, 1).wait_send()

    @pl.when(section > 0)
    def _():
        pipe_copy(section - 1).wait_send()

    @pl.when(seq > 0)
    def _():
        back_copy(seq - 1).wait_send()

    @pl.when(seq < shards - 1)
    def _():
        halo_copy(seq + 1).wait_send()


def on_device(
    section_input, event_ids, lengths, clicks, conversions, conv_weight, type_table, head_weight
):
    inputs_bf = section_input[0, 0]
    rows, width = inputs_bf.shape
    half = rows // 2
    kinds = type_table.shape[1]
    users, shards, sections = (lax.axis_size(name) for name in ("dp", "seq", "pipe"))
    group = users * shards
    share = KERNEL * width // group
    kind_share = kinds // group
    block_rows = share + -(-kind_share // 16) * 16
    vmem = pl.BlockSpec(memory_space=pltpu.VMEM)
    dma = pltpu.SemaphoreType.DMA
    f32, bf16 = jnp.float32, jnp.bfloat16
    conv, kind, grad_in = pl.pallas_call(
        functools.partial(kernel, users, shards, sections, kind_share),
        out_shape=(
            jax.ShapeDtypeStruct((share, width), f32),
            jax.ShapeDtypeStruct((kind_share, width), f32),
            jax.ShapeDtypeStruct((rows, width), bf16),
        ),
        in_specs=[
            vmem, vmem, vmem, vmem, pl.BlockSpec(memory_space=pltpu.SMEM),
            pl.BlockSpec(memory_space=pl.ANY), vmem, vmem,
        ],
        out_specs=(vmem, vmem, vmem),
        scratch_shapes=[
            pltpu.VMEM((KERNEL * width, width), bf16),
            pltpu.VMEM((rows + half, width), f32),
            pltpu.VMEM((KERNEL, rows, width), bf16),
            pltpu.VMEM((KERNEL - 1, rows, width), bf16),
            pltpu.VMEM((group, block_rows, rows), bf16),
            pltpu.VMEM((group, block_rows, rows), bf16),
            pltpu.VMEM((rows, width), f32),
            pltpu.VMEM((rows, width), f32),
            pltpu.VMEM((rows, width), f32),
            pltpu.VMEM((group * rows, width), bf16),
            pltpu.VMEM((half, width), bf16),
            pltpu.VMEM((half, width), bf16),
            pltpu.VMEM((half, width), bf16),
            pltpu.VMEM((rows, width), bf16),
            pltpu.VMEM((rows, width), bf16),
            pltpu.VMEM((8, width), f32),
            dma((KERNEL,)),
            dma((2,)),
            dma((2,)),
            dma((2,)),
            dma((group,)),
            dma((group,)),
            dma((users, 2)),
            dma((users,)),
            dma((users, shards)),
            dma((users, shards)),
        ],
        compiler_params=pltpu.CompilerParams(
            collective_id=0, has_side_effects=True, vmem_limit_bytes=56 * 1024 * 1024
        ),
    )(
        inputs_bf, event_ids, clicks, conversions, lengths, conv_weight[0], type_table[0],
        head_weight,
    )
    return (conv[None], kind[None], grad_in[None, None])


def solution(mesh):
    placed = (
        P("pipe", "dp", "seq", None),
        P("dp", "seq"),
        P("dp"),
        P("dp", "seq"),
        P("dp", "seq"),
        P("pipe", None, None),
        P("pipe", None, None),
        P(),
    )
    return jax.shard_map(
        on_device,
        mesh=mesh,
        in_specs=placed,
        out_specs=(
            P("pipe", ("dp", "seq"), None),
            P("pipe", ("dp", "seq"), None),
            P("pipe", "dp", "seq", None),
        ),
        check_vma=False,
    )
```

```python
import functools

import jax
import jax.numpy as jnp
from jax import lax
from jax.experimental import pallas as pl
from jax.experimental.pallas import tpu as pltpu
from jax.sharding import PartitionSpec as P

KERNEL = 3
EPS = 1e-06
BLOCK = 256
MESH = pl.DeviceIdType.MESH


def kernel(
    users, shards, sections, kind_share,
    x_ref, id_ref, click_ref, convert_ref, length_ref, weight_hbm, table_ref, head_ref,
    conv_ref, type_ref, gin_ref,
    weight_ref, ext, taps, back, tap_src, tap_all, slope, gnorm, gout, gp_all, halo_out, halo_in,
    back_in, inc, gin_buf, heads,
    w_sem, halo_sem, back_sem, pipe_sem, tap_send, tap_recv, dp_send, dp_recv, f_send, f_recv,
):
    rows, width = x_ref.shape
    half = rows // 2
    dp, section, seq = lax.axis_index("dp"), lax.axis_index("pipe"), lax.axis_index("seq")
    group = users * shards
    me = dp * shards + seq
    share = KERNEL * width // group
    is_last = section == sections - 1
    f32, bf16 = jnp.float32, jnp.bfloat16

    for tap in range(KERNEL):
        part = pl.ds(tap * width, width)
        pltpu.make_async_copy(weight_hbm.at[part], weight_ref.at[part], w_sem.at[tap]).start()

    barrier = pltpu.get_barrier_semaphore()

    def peer_id(i):
        peer = lax.rem(me + i, group)
        return peer, lax.div(peer, shards), lax.rem(peer, shards)

    @pl.loop(1, group)
    def _(i):
        _, d, s = peer_id(i)
        pl.semaphore_signal(barrier, inc=1, device_id={"dp": d, "seq": s}, device_id_type=MESH)

    @pl.when(section > 0)
    def _():
        pl.semaphore_signal(barrier, inc=1, device_id={"pipe": section - 1}, device_id_type=MESH)

    @pl.when(section < sections - 1)
    def _():
        pl.semaphore_signal(barrier, inc=1, device_id={"pipe": section + 1}, device_id_type=MESH)

    x = x_ref[...].astype(f32)
    inv = lax.rsqrt(jnp.mean(x * x, axis=-1, keepdims=True) + EPS)
    normed = x * inv
    normed_bf = normed.astype(bf16)
    halo_out[...] = normed_bf[half:]

    pipe_peers = (section > 0).astype(jnp.int32) + (section < sections - 1).astype(jnp.int32)
    pl.semaphore_wait(barrier, group - 1 + pipe_peers)

    def halo_copy(to):
        return pltpu.make_async_remote_copy(
            src_ref=halo_out, dst_ref=halo_in, send_sem=halo_sem.at[0], recv_sem=halo_sem.at[1],
            device_id={"seq": to}, device_id_type=MESH,
        )

    @pl.when(seq < shards - 1)
    def _():
        halo_copy(seq + 1).start()

    ext[half:] = normed_bf.astype(f32)
    taps[0] = normed_bf

    @pl.when(seq == 0)
    def _():
        ext[:half] = jnp.zeros((half, width), f32)

    @pl.when(seq > 0)
    def _():
        halo_copy(seq - 1).wait_recv()
        ext[:half] = halo_in[...].astype(f32)

    def shifted(dest, slot, base, way, tap, cols=slice(None)):
        for place in range(sections):
            start = base + way * tap * (rows // 4 >> place)

            @pl.when(section == place)
            def _():
                dest[slot, :, cols] = ext[start : start + rows, cols].astype(bf16)

    for tap in range(1, KERNEL):
        shifted(taps, tap, half, -1, tap)
    for tap in range(KERNEL):
        part = pl.ds(tap * width, width)
        pltpu.make_async_copy(weight_hbm.at[part], weight_ref.at[part], w_sem.at[tap]).wait()

    id_row = id_ref[...]
    heads[...] = jnp.concatenate(
        [head_ref[...].astype(f32), jnp.zeros((6, width), f32)], axis=0
    )
    kinds = table_ref.shape[0]
    ids = jnp.broadcast_to(id_row, (kinds, rows))
    pick = jnp.where(ids == lax.broadcasted_iota(jnp.int32, (kinds, rows), 0), 1.0, 0.0).astype(f32)
    onehot = jnp.transpose(pick).astype(bf16)

    def forward(i, logits):
        cols = pl.ds(pl.multiple_of(i * BLOCK, BLOCK), BLOCK)
        pre = jnp.dot(onehot, table_ref[:, cols], preferred_element_type=f32)
        for tap in range(KERNEL):
            pre = pre + jnp.dot(
                taps[tap], weight_ref[tap * width : (tap + 1) * width, cols],
                preferred_element_type=f32,
            )
        square = pre * pre
        scale = 0.7978845608028654
        curve = jnp.tanh(scale * (pre + 0.044715 * (square * pre)))
        slope[:, cols] = 0.5 * (1.0 + curve) + 0.5 * pre * (1.0 - curve * curve) * (
            scale * (1.0 + 0.134145 * square)
        )
        out_bf = (x_ref[:, cols].astype(f32) + 0.5 * pre * (1.0 + curve)).astype(bf16)
        return logits + lax.dot_general(
            heads[:, cols].astype(bf16), out_bf, (((1,), (1,)), ((), ())), preferred_element_type=f32
        )

    logits = lax.fori_loop(0, width // BLOCK, forward, jnp.zeros((8, rows), f32))

    def send_taps():
        block_rows = tap_src.shape[1]
        for tap in range(KERNEL):
            weight_rows = jnp.transpose(taps[tap].astype(f32)).astype(bf16)
            low = tap * width
            while low < (tap + 1) * width:
                peer = low // share
                high = min((peer + 1) * share, (tap + 1) * width)
                tap_src[peer, low - peer * share : high - peer * share] = weight_rows[
                    low - tap * width : high - tap * width
                ]
                low = high
        ids_rows = jnp.broadcast_to(id_row.astype(f32), (block_rows - share, rows)).astype(bf16)
        for peer in range(group):
            tap_src[peer, share:] = ids_rows

        @pl.loop(1, group)
        def _(i):
            peer, d, s = peer_id(i)
            pltpu.make_async_remote_copy(
                src_ref=tap_src.at[peer],
                dst_ref=tap_all.at[me],
                send_sem=tap_send.at[peer], recv_sem=tap_recv.at[me],
                device_id={"dp": d, "seq": s}, device_id_type=MESH,
            ).start()
        tap_all[me] = tap_src[me]

    chunks = width // BLOCK

    def pipe_copy(to, c):
        cols = pl.ds(c * BLOCK, BLOCK)
        return pltpu.make_async_remote_copy(
            src_ref=gin_buf.at[:, cols], dst_ref=inc.at[:, cols],
            send_sem=pipe_sem.at[0, c], recv_sem=pipe_sem.at[1, c],
            device_id={"pipe": to}, device_id_type=MESH,
        )

    @pl.when(is_last)
    def _():
        a, b = logits[0:1], logits[1:2]
        y = click_ref[...].astype(f32)
        z = y * convert_ref[...].astype(f32)
        position = seq * rows + lax.broadcasted_iota(jnp.int32, (1, rows), 1)
        m = jnp.where(position < length_ref[0], 1.0, 0.0).astype(f32)
        sa, na = jax.nn.sigmoid(a), jax.nn.sigmoid(-a)
        sb, nb = jax.nn.sigmoid(b), jax.nn.sigmoid(-b)
        rest = (1.0 - z) / (na + sa * nb)
        first = m * ((1.0 - y) * sa - (y + z) * na + rest * (sa * na * sb))
        second = m * (rest * (sa * sb * nb) - z * nb)
        columns = jnp.transpose(
            jnp.concatenate([first, second, jnp.zeros((6, rows), f32)], axis=0)
        )
        gout[...] = columns[:, 0:1] * heads[0:1] + columns[:, 1:2] * heads[1:2]

    @pl.when(section < sections - 1)
    def _():
        send_taps()

    mine = pl.ds(pl.multiple_of(me * rows, rows), rows)

    def back_copy(to, c):
        cols = pl.ds(c * BLOCK, BLOCK)
        return pltpu.make_async_remote_copy(
            src_ref=gp_all.at[pl.ds(pl.multiple_of(me * rows, rows), half), cols],
            dst_ref=back_in.at[:, cols],
            send_sem=back_sem.at[0, c], recv_sem=back_sem.at[1, c],
            device_id={"seq": to}, device_id_type=MESH,
        )

    def line_copy(source, to, way):
        piece = gp_all.at[pl.ds(pl.multiple_of((source * shards + seq) * rows, rows), rows)]
        return pltpu.make_async_remote_copy(
            src_ref=piece, dst_ref=piece, send_sem=dp_send.at[source, way],
            recv_sem=dp_recv.at[source], device_id={"dp": to}, device_id_type=MESH,
        )

    def pass_on(source, left, right):
        if left:

            @pl.when(dp > 0)
            def _():
                line_copy(source, dp - 1, 0).start()

        if right:

            @pl.when(dp < users - 1)
            def _():
                line_copy(source, dp + 1, 1).start()

    def seq_copy(user, source, to):
        piece = gp_all.at[pl.ds(pl.multiple_of((user * shards + source) * rows, rows), rows)]
        return pltpu.make_async_remote_copy(
            src_ref=piece, dst_ref=piece, send_sem=f_send.at[user, to],
            recv_sem=f_recv.at[user, source], device_id={"seq": to}, device_id_type=MESH,
        )

    def times(lhs, tap, c):
        for i in range(chunks):
            out = slice(i * BLOCK, (i + 1) * BLOCK)
            low = tap * width + i * BLOCK
            value = lax.dot_general(
                lhs, weight_ref[low : low + BLOCK, c * BLOCK : (c + 1) * BLOCK],
                (((1,), (1,)), ((), ())), preferred_element_type=f32,
            )
            if tap == 0 and c == 0:
                gnorm[:, out] = value
            else:
                gnorm[:, out] += value

    def later_taps(c):
        cols = slice(c * BLOCK, (c + 1) * BLOCK)

        @pl.when(seq < shards - 1)
        def _():
            back_copy(seq + 1, c).wait_recv()
            ext[rows:, cols] = back_in[:, cols].astype(f32)

        for tap in range(1, KERNEL):
            shifted(back, tap - 1, 0, 1, tap, cols)
            times(back[tap - 1, :, cols], tap, c)

    @pl.when(seq == shards - 1)
    def _():
        ext[rows:] = jnp.zeros((half, width), f32)

    for c in range(chunks):
        cols = slice(c * BLOCK, (c + 1) * BLOCK)

        @pl.when(section < sections - 1)
        def _():
            pipe_copy(section + 1, c).wait_recv()
            gout[:, cols] = inc[:, cols].astype(f32)

        grad_pre = (gout[:, cols] * slope[:, cols]).astype(bf16)
        gp_all[mine, cols] = grad_pre

        @pl.when(seq > 0)
        def _():
            back_copy(seq - 1, c).start()

        if c == chunks - 1:
            pass_on(dp, True, True)
        ext[:rows, cols] = grad_pre.astype(f32)
        times(grad_pre, 0, c)
        if c > 0:
            later_taps(c - 1)
    later_taps(chunks - 1)
    x = x_ref[...].astype(f32)
    inv = lax.rsqrt(jnp.mean(x * x, axis=-1, keepdims=True) + EPS)
    normed = x * inv
    grad_normed = gnorm[...]
    inner = jnp.mean(grad_normed * normed, axis=-1, keepdims=True)
    for c in range(chunks):
        cols = slice(c * BLOCK, (c + 1) * BLOCK)
        gin_buf[:, cols] = (
            gout[:, cols] + inv * (grad_normed[:, cols] - normed[:, cols] * inner)
        ).astype(bf16)

        @pl.when(section > 0)
        def _():
            pipe_copy(section - 1, c).start()

    gin_ref[...] = gin_buf[...]

    @pl.when(is_last)
    def _():
        send_taps()

    def share_out(user):
        @pl.loop(1, shards)
        def _(j):
            seq_copy(user, seq, lax.rem(seq + j, shards)).start()

    share_out(dp)
    conv_ref[...] = jnp.zeros_like(conv_ref)
    type_ref[...] = jnp.zeros_like(type_ref)

    @pl.loop(1, group)
    def _(i):
        peer, d, s = peer_id(i)
        pltpu.make_async_remote_copy(
            src_ref=tap_src.at[peer],
            dst_ref=tap_all.at[peer],
            send_sem=tap_send.at[peer], recv_sem=tap_recv.at[peer],
            device_id={"dp": d, "seq": s}, device_id_type=MESH,
        ).wait()

    kind = me * kind_share + lax.broadcasted_iota(
        jnp.int32, (tap_src.shape[1] - share, rows), 0
    )

    def multiply(user):
        @pl.loop(1, shards)
        def _(j):
            other = lax.rem(seq + j, shards)
            seq_copy(user, other, other).wait()

        pieces = [tap_all[user * shards + s] for s in range(shards)]
        left = jnp.concatenate([piece[:share] for piece in pieces], axis=1)
        picks = jnp.concatenate(
            [
                jnp.where(piece[share:].astype(f32).astype(jnp.int32) == kind, 1.0, 0.0).astype(bf16)
                for piece in pieces
            ],
            axis=1,
        )
        span = pl.ds(pl.multiple_of(user * shards * rows, shards * rows), shards * rows)
        for i in range(width // BLOCK):
            cols = slice(i * BLOCK, (i + 1) * BLOCK)
            right = gp_all[span, cols]
            conv_ref[:, cols] += jnp.dot(left, right, preferred_element_type=f32)
            type_ref[:, cols] += jnp.dot(picks, right, preferred_element_type=f32)[:kind_share]

    @pl.loop(0, users)
    def _(h):
        before, after = dp - h - 1, dp + h + 1

        @pl.when(before >= 0)
        def _():
            line_copy(before, before, 1).wait_recv()
            pass_on(before, False, True)
            share_out(before)

        @pl.when(after < users)
        def _():
            line_copy(after, after, 0).wait_recv()
            pass_on(after, True, False)
            share_out(after)

        @pl.when(dp - h >= 0)
        def _():
            multiply(dp - h)

        @pl.when((h > 0) & (dp + h < users))
        def _():
            multiply(dp + h)

    @pl.loop(0, users)
    def _(source):
        @pl.when((source >= dp) & (dp > 0))
        def _():
            line_copy(source, dp - 1, 0).wait_send()

        @pl.when((source <= dp) & (dp < users - 1))
        def _():
            line_copy(source, dp + 1, 1).wait_send()

    @pl.when(section > 0)
    def _():
        for c in range(chunks):
            pipe_copy(section - 1, c).wait_send()

    @pl.when(seq > 0)
    def _():
        for c in range(chunks):
            back_copy(seq - 1, c).wait_send()

    @pl.when(seq < shards - 1)
    def _():
        halo_copy(seq + 1).wait_send()


def on_device(
    section_input, event_ids, lengths, clicks, conversions, conv_weight, type_table, head_weight
):
    inputs_bf = section_input[0, 0]
    rows, width = inputs_bf.shape
    half = rows // 2
    kinds = type_table.shape[1]
    users, shards, sections = (lax.axis_size(name) for name in ("dp", "seq", "pipe"))
    group = users * shards
    share = KERNEL * width // group
    kind_share = kinds // group
    block_rows = share + -(-kind_share // 16) * 16
    vmem = pl.BlockSpec(memory_space=pltpu.VMEM)
    dma = pltpu.SemaphoreType.DMA
    f32, bf16 = jnp.float32, jnp.bfloat16
    conv, kind, grad_in = pl.pallas_call(
        functools.partial(kernel, users, shards, sections, kind_share),
        out_shape=(
            jax.ShapeDtypeStruct((share, width), f32),
            jax.ShapeDtypeStruct((kind_share, width), f32),
            jax.ShapeDtypeStruct((rows, width), bf16),
        ),
        in_specs=[
            vmem, vmem, vmem, vmem, pl.BlockSpec(memory_space=pltpu.SMEM),
            pl.BlockSpec(memory_space=pltpu.HBM), vmem, vmem,
        ],
        out_specs=(vmem, vmem, vmem),
        scratch_shapes=[
            pltpu.VMEM((KERNEL * width, width), bf16),
            pltpu.VMEM((rows + half, width), f32),
            pltpu.VMEM((KERNEL, rows, width), bf16),
            pltpu.VMEM((KERNEL - 1, rows, width), bf16),
            pltpu.VMEM((group, block_rows, rows), bf16),
            pltpu.VMEM((group, block_rows, rows), bf16),
            pltpu.VMEM((rows, width), f32),
            pltpu.VMEM((rows, width), f32),
            pltpu.VMEM((rows, width), f32),
            pltpu.VMEM((group * rows, width), bf16),
            pltpu.VMEM((half, width), bf16),
            pltpu.VMEM((half, width), bf16),
            pltpu.VMEM((half, width), bf16),
            pltpu.VMEM((rows, width), bf16),
            pltpu.VMEM((rows, width), bf16),
            pltpu.VMEM((8, width), f32),
            dma((KERNEL,)),
            dma((2,)),
            dma((2, width // BLOCK)),
            dma((2, width // BLOCK)),
            dma((group,)),
            dma((group,)),
            dma((users, 2)),
            dma((users,)),
            dma((users, shards)),
            dma((users, shards)),
        ],
        compiler_params=pltpu.CompilerParams(
            collective_id=0, has_side_effects=True, vmem_limit_bytes=58 * 1024 * 1024
        ),
    )(
        inputs_bf, event_ids, clicks, conversions, lengths, conv_weight[0], type_table[0],
        head_weight,
    )
    return (conv[None], kind[None], grad_in[None, None])


def solution(mesh):
    placed = (
        P("pipe", "dp", "seq", None),
        P("dp", "seq"),
        P("dp"),
        P("dp", "seq"),
        P("dp", "seq"),
        P("pipe", None, None),
        P("pipe", None, None),
        P(),
    )
    return jax.shard_map(
        on_device,
        mesh=mesh,
        in_specs=placed,
        out_specs=(
            P("pipe", ("dp", "seq"), None),
            P("pipe", ("dp", "seq"), None),
            P("pipe", "dp", "seq", None),
        ),
        check_vma=False,
    )
```

```python
import functools

import jax
import jax.numpy as jnp
from jax import lax
from jax.experimental import pallas as pl
from jax.experimental.pallas import tpu as pltpu
from jax.sharding import PartitionSpec as P

KERNEL = 3
EPS = 1e-06
BLOCK = 256
MESH = pl.DeviceIdType.MESH


def kernel(
    users, shards, sections, kind_share,
    x_ref, id_ref, click_ref, convert_ref, length_ref, weight_hbm, table_ref, head_ref,
    conv_ref, type_ref, gin_ref,
    weight_ref, ext, taps, back, tap_src, tap_all, slope, gnorm, gout, gp_all, halo_out, halo_in,
    back_in, inc, gin_buf, heads,
    w_sem, halo_sem, back_sem, pipe_sem, tap_send, tap_recv, dp_send, dp_recv, f_send, f_recv,
):
    rows, width = x_ref.shape
    half = rows // 2
    dp, section, seq = lax.axis_index("dp"), lax.axis_index("pipe"), lax.axis_index("seq")
    group = users * shards
    me = dp * shards + seq
    share = KERNEL * width // group
    is_last = section == sections - 1
    f32, bf16 = jnp.float32, jnp.bfloat16

    for tap in range(KERNEL):
        part = pl.ds(tap * width, width)
        pltpu.make_async_copy(weight_hbm.at[part], weight_ref.at[part], w_sem.at[tap]).start()

    barrier = pltpu.get_barrier_semaphore()

    def peer_id(i):
        peer = lax.rem(me + i, group)
        return peer, lax.div(peer, shards), lax.rem(peer, shards)

    @pl.loop(1, group)
    def _(i):
        _, d, s = peer_id(i)
        pl.semaphore_signal(barrier, inc=1, device_id={"dp": d, "seq": s}, device_id_type=MESH)

    @pl.when(section > 0)
    def _():
        pl.semaphore_signal(barrier, inc=1, device_id={"pipe": section - 1}, device_id_type=MESH)

    @pl.when(section < sections - 1)
    def _():
        pl.semaphore_signal(barrier, inc=1, device_id={"pipe": section + 1}, device_id_type=MESH)

    x = x_ref[...].astype(f32)
    inv = lax.rsqrt(jnp.mean(x * x, axis=-1, keepdims=True) + EPS)
    normed = x * inv
    normed_bf = normed.astype(bf16)
    halo_out[...] = normed_bf[half:]

    pipe_peers = (section > 0).astype(jnp.int32) + (section < sections - 1).astype(jnp.int32)
    pl.semaphore_wait(barrier, group - 1 + pipe_peers)

    def halo_copy(to):
        return pltpu.make_async_remote_copy(
            src_ref=halo_out, dst_ref=halo_in, send_sem=halo_sem.at[0], recv_sem=halo_sem.at[1],
            device_id={"seq": to}, device_id_type=MESH,
        )

    @pl.when(seq < shards - 1)
    def _():
        halo_copy(seq + 1).start()

    ext[half:] = normed_bf.astype(f32)
    taps[0] = normed_bf

    @pl.when(seq == 0)
    def _():
        ext[:half] = jnp.zeros((half, width), f32)

    @pl.when(seq > 0)
    def _():
        halo_copy(seq - 1).wait_recv()
        ext[:half] = halo_in[...].astype(f32)

    def shifted(dest, slot, base, way, tap, cols=slice(None)):
        for place in range(sections):
            start = base + way * tap * (rows // 4 >> place)

            @pl.when(section == place)
            def _():
                dest[slot, :, cols] = ext[start : start + rows, cols].astype(bf16)

    for tap in range(1, KERNEL):
        shifted(taps, tap, half, -1, tap)
    for tap in range(KERNEL):
        part = pl.ds(tap * width, width)
        pltpu.make_async_copy(weight_hbm.at[part], weight_ref.at[part], w_sem.at[tap]).wait()

    id_row = id_ref[...]
    heads[...] = jnp.concatenate(
        [head_ref[...].astype(f32), jnp.zeros((6, width), f32)], axis=0
    )
    kinds = table_ref.shape[0]
    ids = jnp.broadcast_to(id_row, (kinds, rows))
    pick = jnp.where(ids == lax.broadcasted_iota(jnp.int32, (kinds, rows), 0), 1.0, 0.0).astype(f32)
    onehot = jnp.transpose(pick).astype(bf16)

    def forward(i, logits):
        cols = pl.ds(pl.multiple_of(i * BLOCK, BLOCK), BLOCK)
        pre = jnp.dot(onehot, table_ref[:, cols], preferred_element_type=f32)
        for tap in range(KERNEL):
            pre = pre + jnp.dot(
                taps[tap], weight_ref[tap * width : (tap + 1) * width, cols],
                preferred_element_type=f32,
            )
        square = pre * pre
        scale = 0.7978845608028654
        curve = jnp.tanh(scale * (pre + 0.044715 * (square * pre)))
        slope[:, cols] = 0.5 * (1.0 + curve) + 0.5 * pre * (1.0 - curve * curve) * (
            scale * (1.0 + 0.134145 * square)
        )
        out_bf = (x_ref[:, cols].astype(f32) + 0.5 * pre * (1.0 + curve)).astype(bf16)
        return logits + lax.dot_general(
            heads[:, cols].astype(bf16), out_bf, (((1,), (1,)), ((), ())), preferred_element_type=f32
        )

    logits = lax.fori_loop(0, width // BLOCK, forward, jnp.zeros((8, rows), f32))

    def send_taps():
        block_rows = tap_src.shape[1]
        for tap in range(KERNEL):
            weight_rows = jnp.transpose(taps[tap].astype(f32)).astype(bf16)
            low = tap * width
            while low < (tap + 1) * width:
                peer = low // share
                high = min((peer + 1) * share, (tap + 1) * width)
                tap_src[peer, low - peer * share : high - peer * share] = weight_rows[
                    low - tap * width : high - tap * width
                ]
                low = high
        ids_rows = jnp.broadcast_to(id_row.astype(f32), (block_rows - share, rows)).astype(bf16)
        for peer in range(group):
            tap_src[peer, share:] = ids_rows

        @pl.loop(1, group)
        def _(i):
            peer, d, s = peer_id(i)
            pltpu.make_async_remote_copy(
                src_ref=tap_src.at[peer],
                dst_ref=tap_all.at[me],
                send_sem=tap_send.at[peer], recv_sem=tap_recv.at[me],
                device_id={"dp": d, "seq": s}, device_id_type=MESH,
            ).start()
        tap_all[me] = tap_src[me]

    chunks = width // BLOCK

    def pipe_copy(to, c):
        cols = pl.ds(c * BLOCK, BLOCK)
        return pltpu.make_async_remote_copy(
            src_ref=gin_buf.at[:, cols], dst_ref=inc.at[:, cols],
            send_sem=pipe_sem.at[0, c], recv_sem=pipe_sem.at[1, c],
            device_id={"pipe": to}, device_id_type=MESH,
        )

    @pl.when(is_last)
    def _():
        a, b = logits[0:1], logits[1:2]
        y = click_ref[...].astype(f32)
        z = y * convert_ref[...].astype(f32)
        position = seq * rows + lax.broadcasted_iota(jnp.int32, (1, rows), 1)
        m = jnp.where(position < length_ref[0], 1.0, 0.0).astype(f32)
        sa, na = jax.nn.sigmoid(a), jax.nn.sigmoid(-a)
        sb, nb = jax.nn.sigmoid(b), jax.nn.sigmoid(-b)
        rest = (1.0 - z) / (na + sa * nb)
        first = m * ((1.0 - y) * sa - (y + z) * na + rest * (sa * na * sb))
        second = m * (rest * (sa * sb * nb) - z * nb)
        columns = jnp.transpose(
            jnp.concatenate([first, second, jnp.zeros((6, rows), f32)], axis=0)
        )
        gout[...] = columns[:, 0:1] * heads[0:1] + columns[:, 1:2] * heads[1:2]

    @pl.when(section < sections - 1)
    def _():
        send_taps()

    mine = pl.ds(pl.multiple_of(me * rows, rows), rows)

    def back_copy(to, c):
        cols = pl.ds(c * BLOCK, BLOCK)
        return pltpu.make_async_remote_copy(
            src_ref=gp_all.at[pl.ds(pl.multiple_of(me * rows, rows), half), cols],
            dst_ref=back_in.at[:, cols],
            send_sem=back_sem.at[0, c], recv_sem=back_sem.at[1, c],
            device_id={"seq": to}, device_id_type=MESH,
        )

    def line_copy(source, to, way):
        piece = gp_all.at[pl.ds(pl.multiple_of((source * shards + seq) * rows, rows), rows)]
        return pltpu.make_async_remote_copy(
            src_ref=piece, dst_ref=piece, send_sem=dp_send.at[source, way],
            recv_sem=dp_recv.at[source], device_id={"dp": to}, device_id_type=MESH,
        )

    def pass_on(source, left, right):
        if left:

            @pl.when(dp > 0)
            def _():
                line_copy(source, dp - 1, 0).start()

        if right:

            @pl.when(dp < users - 1)
            def _():
                line_copy(source, dp + 1, 1).start()

    def seq_copy(user, source, to):
        piece = gp_all.at[pl.ds(pl.multiple_of((user * shards + source) * rows, rows), rows)]
        return pltpu.make_async_remote_copy(
            src_ref=piece, dst_ref=piece, send_sem=f_send.at[user, to],
            recv_sem=f_recv.at[user, source], device_id={"seq": to}, device_id_type=MESH,
        )

    def times(lhs, tap, c):
        for i in range(chunks):
            out = slice(i * BLOCK, (i + 1) * BLOCK)
            low = tap * width + i * BLOCK
            value = lax.dot_general(
                lhs, weight_ref[low : low + BLOCK, c * BLOCK : (c + 1) * BLOCK],
                (((1,), (1,)), ((), ())), preferred_element_type=f32,
            )
            if tap == 0 and c == 0:
                gnorm[:, out] = value
            else:
                gnorm[:, out] += value

    def later_taps(c):
        cols = slice(c * BLOCK, (c + 1) * BLOCK)

        @pl.when(seq < shards - 1)
        def _():
            back_copy(seq + 1, c).wait_recv()
            ext[rows:, cols] = back_in[:, cols].astype(f32)

        for tap in range(1, KERNEL):
            shifted(back, tap - 1, 0, 1, tap, cols)
            times(back[tap - 1, :, cols], tap, c)

    @pl.when(seq == shards - 1)
    def _():
        ext[rows:] = jnp.zeros((half, width), f32)

    for c in range(chunks):
        cols = slice(c * BLOCK, (c + 1) * BLOCK)

        @pl.when(section < sections - 1)
        def _():
            pipe_copy(section + 1, c).wait_recv()
            gout[:, cols] = inc[:, cols].astype(f32)

        grad_pre = (gout[:, cols] * slope[:, cols]).astype(bf16)
        gp_all[mine, cols] = grad_pre

        @pl.when(seq > 0)
        def _():
            back_copy(seq - 1, c).start()

        if c == chunks - 1:
            pass_on(dp, True, True)
        ext[:rows, cols] = grad_pre.astype(f32)
        times(grad_pre, 0, c)
        if c > 0:
            later_taps(c - 1)
    later_taps(chunks - 1)
    x = x_ref[...].astype(f32)
    inv = lax.rsqrt(jnp.mean(x * x, axis=-1, keepdims=True) + EPS)
    normed = x * inv
    grad_normed = gnorm[...]
    inner = jnp.mean(grad_normed * normed, axis=-1, keepdims=True)
    for c in range(chunks):
        cols = slice(c * BLOCK, (c + 1) * BLOCK)
        gin_buf[:, cols] = (
            gout[:, cols] + inv * (grad_normed[:, cols] - normed[:, cols] * inner)
        ).astype(bf16)

        @pl.when(section > 0)
        def _():
            pipe_copy(section - 1, c).start()

    gin_ref[...] = gin_buf[...]

    @pl.when(is_last)
    def _():
        send_taps()

    def share_out(user):
        @pl.loop(1, shards)
        def _(j):
            seq_copy(user, seq, lax.rem(seq + j, shards)).start()

    share_out(dp)
    conv_ref[...] = jnp.zeros_like(conv_ref)
    type_ref[...] = jnp.zeros_like(type_ref)

    @pl.loop(1, group)
    def _(i):
        peer, d, s = peer_id(i)
        pltpu.make_async_remote_copy(
            src_ref=tap_src.at[peer],
            dst_ref=tap_all.at[peer],
            send_sem=tap_send.at[peer], recv_sem=tap_recv.at[peer],
            device_id={"dp": d, "seq": s}, device_id_type=MESH,
        ).wait()

    kind = me * kind_share + lax.broadcasted_iota(
        jnp.int32, (tap_src.shape[1] - share, rows), 0
    )

    def multiply(user):
        @pl.loop(1, shards)
        def _(j):
            other = lax.rem(seq + j, shards)
            seq_copy(user, other, other).wait()

        pieces = [tap_all[user * shards + s] for s in range(shards)]
        left = jnp.concatenate([piece[:share] for piece in pieces], axis=1)
        picks = jnp.concatenate(
            [
                jnp.where(piece[share:].astype(f32).astype(jnp.int32) == kind, 1.0, 0.0).astype(bf16)
                for piece in pieces
            ],
            axis=1,
        )
        span = pl.ds(pl.multiple_of(user * shards * rows, shards * rows), shards * rows)
        for i in range(width // BLOCK):
            cols = slice(i * BLOCK, (i + 1) * BLOCK)
            right = gp_all[span, cols]
            conv_ref[:, cols] += jnp.dot(left, right, preferred_element_type=f32)
            type_ref[:, cols] += jnp.dot(picks, right, preferred_element_type=f32)[:kind_share]

    @pl.loop(0, users)
    def _(h):
        before, after = dp - h - 1, dp + h + 1

        @pl.when(before >= 0)
        def _():
            line_copy(before, before, 1).wait_recv()
            pass_on(before, False, True)
            share_out(before)

        @pl.when(after < users)
        def _():
            line_copy(after, after, 0).wait_recv()
            pass_on(after, True, False)
            share_out(after)

        @pl.when(dp - h >= 0)
        def _():
            multiply(dp - h)

        @pl.when((h > 0) & (dp + h < users))
        def _():
            multiply(dp + h)

    @pl.loop(0, users)
    def _(source):
        @pl.when((source >= dp) & (dp > 0))
        def _():
            line_copy(source, dp - 1, 0).wait_send()

        @pl.when((source <= dp) & (dp < users - 1))
        def _():
            line_copy(source, dp + 1, 1).wait_send()

    @pl.when(section > 0)
    def _():
        for c in range(chunks):
            pipe_copy(section - 1, c).wait_send()

    @pl.when(seq > 0)
    def _():
        for c in range(chunks):
            back_copy(seq - 1, c).wait_send()

    @pl.when(seq < shards - 1)
    def _():
        halo_copy(seq + 1).wait_send()


def on_device(
    section_input, event_ids, lengths, clicks, conversions, conv_weight, type_table, head_weight
):
    inputs_bf = section_input[0, 0]
    rows, width = inputs_bf.shape
    half = rows // 2
    kinds = type_table.shape[1]
    users, shards, sections = (lax.axis_size(name) for name in ("dp", "seq", "pipe"))
    group = users * shards
    share = KERNEL * width // group
    kind_share = kinds // group
    block_rows = share + -(-kind_share // 16) * 16
    vmem = pl.BlockSpec(memory_space=pltpu.VMEM)
    dma = pltpu.SemaphoreType.DMA
    f32, bf16 = jnp.float32, jnp.bfloat16
    conv, kind, grad_in = pl.pallas_call(
        functools.partial(kernel, users, shards, sections, kind_share),
        out_shape=(
            jax.ShapeDtypeStruct((share, width), f32),
            jax.ShapeDtypeStruct((kind_share, width), f32),
            jax.ShapeDtypeStruct((rows, width), bf16),
        ),
        in_specs=[
            vmem, vmem, vmem, vmem, pl.BlockSpec(memory_space=pltpu.SMEM),
            pl.BlockSpec(memory_space=pltpu.HBM), vmem, vmem,
        ],
        out_specs=(vmem, vmem, vmem),
        scratch_shapes=[
            pltpu.VMEM((KERNEL * width, width), bf16),
            pltpu.VMEM((rows + half, width), f32),
            pltpu.VMEM((KERNEL, rows, width), bf16),
            pltpu.VMEM((KERNEL - 1, rows, width), bf16),
            pltpu.VMEM((group, block_rows, rows), bf16),
            pltpu.VMEM((group, block_rows, rows), bf16),
            pltpu.VMEM((rows, width), f32),
            pltpu.VMEM((rows, width), f32),
            pltpu.VMEM((rows, width), f32),
            pltpu.VMEM((group * rows, width), bf16),
            pltpu.VMEM((half, width), bf16),
            pltpu.VMEM((half, width), bf16),
            pltpu.VMEM((half, width), bf16),
            pltpu.VMEM((rows, width), bf16),
            pltpu.VMEM((rows, width), bf16),
            pltpu.VMEM((8, width), f32),
            dma((KERNEL,)),
            dma((2,)),
            dma((2, width // BLOCK)),
            dma((2, width // BLOCK)),
            dma((group,)),
            dma((group,)),
            dma((users, 2)),
            dma((users,)),
            dma((users, shards)),
            dma((users, shards)),
        ],
        compiler_params=pltpu.CompilerParams(
            collective_id=0, has_side_effects=True, vmem_limit_bytes=46 * 1024 * 1024
        ),
    )(
        inputs_bf, event_ids, clicks, conversions, lengths, conv_weight[0], type_table[0],
        head_weight,
    )
    return (conv[None], kind[None], grad_in[None, None])


def solution(mesh):
    placed = (
        P("pipe", "dp", "seq", None),
        P("dp", "seq"),
        P("dp"),
        P("dp", "seq"),
        P("dp", "seq"),
        P("pipe", None, None),
        P("pipe", None, None),
        P(),
    )
    return jax.shard_map(
        on_device,
        mesh=mesh,
        in_specs=placed,
        out_specs=(
            P("pipe", ("dp", "seq"), None),
            P("pipe", ("dp", "seq"), None),
            P("pipe", "dp", "seq", None),
        ),
        check_vma=False,
    )
```

```python
import functools

import jax
import jax.numpy as jnp
from jax import lax
from jax.experimental import pallas as pl
from jax.experimental.pallas import tpu as pltpu
from jax.sharding import PartitionSpec as P

KERNEL = 3
EPS = 1e-06
BLOCK = 256
MESH = pl.DeviceIdType.MESH


def kernel(
    users, shards, sections, kind_share,
    x_ref, id_ref, click_ref, convert_ref, length_ref, weight_hbm, table_ref, head_ref,
    conv_ref, type_ref, gin_ref,
    weight_ref, ext, taps, back, tap_src, tap_all, slope, gnorm, gout, gp_all, halo_out, halo_in,
    back_in, inc, gin_buf, heads,
    w_sem, halo_sem, back_sem, pipe_sem, tap_send, tap_recv, dp_send, dp_recv, f_send, f_recv,
):
    rows, width = x_ref.shape
    half = rows // 2
    dp, section, seq = lax.axis_index("dp"), lax.axis_index("pipe"), lax.axis_index("seq")
    group = users * shards
    me = dp * shards + seq
    share = KERNEL * width // group
    is_last = section == sections - 1
    f32, bf16 = jnp.float32, jnp.bfloat16

    for tap in range(KERNEL):
        part = pl.ds(tap * width, width)
        pltpu.make_async_copy(weight_hbm.at[part], weight_ref.at[part], w_sem.at[tap]).start()

    barrier = pltpu.get_barrier_semaphore()

    def peer_id(i):
        peer = lax.rem(me + i, group)
        return peer, lax.div(peer, shards), lax.rem(peer, shards)

    @pl.loop(1, group)
    def _(i):
        _, d, s = peer_id(i)
        pl.semaphore_signal(barrier, inc=1, device_id={"dp": d, "seq": s}, device_id_type=MESH)

    @pl.when(section > 0)
    def _():
        pl.semaphore_signal(barrier, inc=1, device_id={"pipe": section - 1}, device_id_type=MESH)

    @pl.when(section < sections - 1)
    def _():
        pl.semaphore_signal(barrier, inc=1, device_id={"pipe": section + 1}, device_id_type=MESH)

    x = x_ref[...].astype(f32)
    inv = lax.rsqrt(jnp.mean(x * x, axis=-1, keepdims=True) + EPS)
    normed = x * inv
    normed_bf = normed.astype(bf16)
    halo_out[...] = normed_bf[half:]

    pipe_peers = (section > 0).astype(jnp.int32) + (section < sections - 1).astype(jnp.int32)
    pl.semaphore_wait(barrier, group - 1 + pipe_peers)

    def halo_copy(to):
        return pltpu.make_async_remote_copy(
            src_ref=halo_out, dst_ref=halo_in, send_sem=halo_sem.at[0], recv_sem=halo_sem.at[1],
            device_id={"seq": to}, device_id_type=MESH,
        )

    @pl.when(seq < shards - 1)
    def _():
        halo_copy(seq + 1).start()

    ext[half:] = normed_bf.astype(f32)
    taps[0] = normed_bf

    @pl.when(seq == 0)
    def _():
        ext[:half] = jnp.zeros((half, width), f32)

    @pl.when(seq > 0)
    def _():
        halo_copy(seq - 1).wait_recv()
        ext[:half] = halo_in[...].astype(f32)

    def shifted(dest, slot, base, way, tap, cols=slice(None)):
        for place in range(sections):
            start = base + way * tap * (rows // 4 >> place)

            @pl.when(section == place)
            def _():
                dest[slot, :, cols] = ext[start : start + rows, cols].astype(bf16)

    for tap in range(1, KERNEL):
        shifted(taps, tap, half, -1, tap)
    for tap in range(KERNEL):
        part = pl.ds(tap * width, width)
        pltpu.make_async_copy(weight_hbm.at[part], weight_ref.at[part], w_sem.at[tap]).wait()

    id_row = id_ref[...]
    heads[...] = jnp.concatenate(
        [head_ref[...].astype(f32), jnp.zeros((6, width), f32)], axis=0
    )
    kinds = table_ref.shape[0]
    ids = jnp.broadcast_to(id_row, (kinds, rows))
    pick = jnp.where(ids == lax.broadcasted_iota(jnp.int32, (kinds, rows), 0), 1.0, 0.0).astype(f32)
    onehot = jnp.transpose(pick).astype(bf16)

    def forward(i, logits):
        cols = pl.ds(pl.multiple_of(i * BLOCK, BLOCK), BLOCK)
        pre = jnp.dot(onehot, table_ref[:, cols], preferred_element_type=f32)
        for tap in range(KERNEL):
            pre = pre + jnp.dot(
                taps[tap], weight_ref[tap * width : (tap + 1) * width, cols],
                preferred_element_type=f32,
            )
        square = pre * pre
        scale = 0.7978845608028654
        curve = jnp.tanh(scale * (pre + 0.044715 * (square * pre)))
        slope[:, cols] = 0.5 * (1.0 + curve) + 0.5 * pre * (1.0 - curve * curve) * (
            scale * (1.0 + 0.134145 * square)
        )
        out_bf = (x_ref[:, cols].astype(f32) + 0.5 * pre * (1.0 + curve)).astype(bf16)
        return logits + lax.dot_general(
            heads[:, cols].astype(bf16), out_bf, (((1,), (1,)), ((), ())), preferred_element_type=f32
        )

    logits = lax.fori_loop(0, width // BLOCK, forward, jnp.zeros((8, rows), f32))

    def send_taps():
        block_rows = tap_src.shape[1]
        for tap in range(KERNEL):
            weight_rows = jnp.transpose(taps[tap].astype(f32)).astype(bf16)
            low = tap * width
            while low < (tap + 1) * width:
                peer = low // share
                high = min((peer + 1) * share, (tap + 1) * width)
                tap_src[peer, low - peer * share : high - peer * share] = weight_rows[
                    low - tap * width : high - tap * width
                ]
                low = high
        ids_rows = jnp.broadcast_to(id_row.astype(f32), (block_rows - share, rows)).astype(bf16)
        for peer in range(group):
            tap_src[peer, share:] = ids_rows

        @pl.loop(1, group)
        def _(i):
            peer, d, s = peer_id(i)
            pltpu.make_async_remote_copy(
                src_ref=tap_src.at[peer],
                dst_ref=tap_all.at[me],
                send_sem=tap_send.at[peer], recv_sem=tap_recv.at[me],
                device_id={"dp": d, "seq": s}, device_id_type=MESH,
            ).start()
        tap_all[me] = tap_src[me]

    chunks = width // BLOCK

    def pipe_copy(to, c):
        cols = pl.ds(c * BLOCK, BLOCK)
        return pltpu.make_async_remote_copy(
            src_ref=gin_buf.at[:, cols], dst_ref=inc.at[:, cols],
            send_sem=pipe_sem.at[0, c], recv_sem=pipe_sem.at[1, c],
            device_id={"pipe": to}, device_id_type=MESH,
        )

    @pl.when(is_last)
    def _():
        a, b = logits[0:1], logits[1:2]
        y = click_ref[...].astype(f32)
        z = y * convert_ref[...].astype(f32)
        position = seq * rows + lax.broadcasted_iota(jnp.int32, (1, rows), 1)
        m = jnp.where(position < length_ref[0], 1.0, 0.0).astype(f32)
        sa, na = jax.nn.sigmoid(a), jax.nn.sigmoid(-a)
        sb, nb = jax.nn.sigmoid(b), jax.nn.sigmoid(-b)
        rest = (1.0 - z) / (na + sa * nb)
        first = m * ((1.0 - y) * sa - (y + z) * na + rest * (sa * na * sb))
        second = m * (rest * (sa * sb * nb) - z * nb)
        columns = jnp.transpose(
            jnp.concatenate([first, second, jnp.zeros((6, rows), f32)], axis=0)
        )
        gout[...] = columns[:, 0:1] * heads[0:1] + columns[:, 1:2] * heads[1:2]

    @pl.when(section < sections - 1)
    def _():
        send_taps()
        conv_ref[...] = jnp.zeros_like(conv_ref)
        type_ref[...] = jnp.zeros_like(type_ref)

    def share_out(user):
        @pl.loop(1, shards)
        def _(j):
            seq_copy(user, seq, lax.rem(seq + j, shards)).start()

    mine = pl.ds(pl.multiple_of(me * rows, rows), rows)

    def back_copy(to, c):
        cols = pl.ds(c * BLOCK, BLOCK)
        return pltpu.make_async_remote_copy(
            src_ref=gp_all.at[pl.ds(pl.multiple_of(me * rows, rows), half), cols],
            dst_ref=back_in.at[:, cols],
            send_sem=back_sem.at[0, c], recv_sem=back_sem.at[1, c],
            device_id={"seq": to}, device_id_type=MESH,
        )

    def line_copy(source, to, way):
        piece = gp_all.at[pl.ds(pl.multiple_of((source * shards + seq) * rows, rows), rows)]
        return pltpu.make_async_remote_copy(
            src_ref=piece, dst_ref=piece, send_sem=dp_send.at[source, way],
            recv_sem=dp_recv.at[source], device_id={"dp": to}, device_id_type=MESH,
        )

    def pass_on(source, left, right):
        if left:

            @pl.when(dp > 0)
            def _():
                line_copy(source, dp - 1, 0).start()

        if right:

            @pl.when(dp < users - 1)
            def _():
                line_copy(source, dp + 1, 1).start()

    def seq_copy(user, source, to):
        piece = gp_all.at[pl.ds(pl.multiple_of((user * shards + source) * rows, rows), rows)]
        return pltpu.make_async_remote_copy(
            src_ref=piece, dst_ref=piece, send_sem=f_send.at[user, to],
            recv_sem=f_recv.at[user, source], device_id={"seq": to}, device_id_type=MESH,
        )

    def times(lhs, tap, c):
        for i in range(chunks):
            out = slice(i * BLOCK, (i + 1) * BLOCK)
            low = tap * width + i * BLOCK
            value = lax.dot_general(
                lhs, weight_ref[low : low + BLOCK, c * BLOCK : (c + 1) * BLOCK],
                (((1,), (1,)), ((), ())), preferred_element_type=f32,
            )
            if tap == 0 and c == 0:
                gnorm[:, out] = value
            else:
                gnorm[:, out] += value

    def later_taps(c):
        cols = slice(c * BLOCK, (c + 1) * BLOCK)

        @pl.when(seq < shards - 1)
        def _():
            back_copy(seq + 1, c).wait_recv()
            ext[rows:, cols] = back_in[:, cols].astype(f32)

        for tap in range(1, KERNEL):
            shifted(back, tap - 1, 0, 1, tap, cols)
            times(back[tap - 1, :, cols], tap, c)

    @pl.when(seq == shards - 1)
    def _():
        ext[rows:] = jnp.zeros((half, width), f32)

    for c in range(chunks):
        cols = slice(c * BLOCK, (c + 1) * BLOCK)

        @pl.when(section < sections - 1)
        def _():
            pipe_copy(section + 1, c).wait_recv()
            gout[:, cols] = inc[:, cols].astype(f32)

        grad_pre = (gout[:, cols] * slope[:, cols]).astype(bf16)
        gp_all[mine, cols] = grad_pre

        @pl.when(seq > 0)
        def _():
            back_copy(seq - 1, c).start()

        if c == chunks - 1:
            pass_on(dp, True, True)
        ext[:rows, cols] = grad_pre.astype(f32)
        times(grad_pre, 0, c)
        if c > 0:
            later_taps(c - 1)
    later_taps(chunks - 1)
    share_out(dp)
    x = x_ref[...].astype(f32)
    inv = lax.rsqrt(jnp.mean(x * x, axis=-1, keepdims=True) + EPS)
    normed = x * inv
    grad_normed = gnorm[...]
    inner = jnp.mean(grad_normed * normed, axis=-1, keepdims=True)
    for c in range(chunks):
        cols = slice(c * BLOCK, (c + 1) * BLOCK)
        gin_buf[:, cols] = (
            gout[:, cols] + inv * (grad_normed[:, cols] - normed[:, cols] * inner)
        ).astype(bf16)

        @pl.when(section > 0)
        def _():
            pipe_copy(section - 1, c).start()

    gin_ref[...] = gin_buf[...]

    @pl.when(is_last)
    def _():
        send_taps()
        conv_ref[...] = jnp.zeros_like(conv_ref)
        type_ref[...] = jnp.zeros_like(type_ref)


    @pl.loop(1, group)
    def _(i):
        peer, d, s = peer_id(i)
        pltpu.make_async_remote_copy(
            src_ref=tap_src.at[peer],
            dst_ref=tap_all.at[peer],
            send_sem=tap_send.at[peer], recv_sem=tap_recv.at[peer],
            device_id={"dp": d, "seq": s}, device_id_type=MESH,
        ).wait()

    kind = me * kind_share + lax.broadcasted_iota(
        jnp.int32, (tap_src.shape[1] - share, rows), 0
    )

    def multiply(user):
        @pl.loop(1, shards)
        def _(j):
            other = lax.rem(seq + j, shards)
            seq_copy(user, other, other).wait()

        pieces = [tap_all[user * shards + s] for s in range(shards)]
        left = jnp.concatenate([piece[:share] for piece in pieces], axis=1)
        picks = jnp.concatenate(
            [
                jnp.where(piece[share:].astype(f32).astype(jnp.int32) == kind, 1.0, 0.0).astype(bf16)
                for piece in pieces
            ],
            axis=1,
        )
        span = pl.ds(pl.multiple_of(user * shards * rows, shards * rows), shards * rows)
        for i in range(width // BLOCK):
            cols = slice(i * BLOCK, (i + 1) * BLOCK)
            right = gp_all[span, cols]
            conv_ref[:, cols] += jnp.dot(left, right, preferred_element_type=f32)
            type_ref[:, cols] += jnp.dot(picks, right, preferred_element_type=f32)[:kind_share]

    @pl.loop(0, users)
    def _(h):
        before, after = dp - h - 1, dp + h + 1

        @pl.when(before >= 0)
        def _():
            line_copy(before, before, 1).wait_recv()
            pass_on(before, False, True)
            share_out(before)

        @pl.when(after < users)
        def _():
            line_copy(after, after, 0).wait_recv()
            pass_on(after, True, False)
            share_out(after)

        @pl.when(dp - h >= 0)
        def _():
            multiply(dp - h)

        @pl.when((h > 0) & (dp + h < users))
        def _():
            multiply(dp + h)

    @pl.loop(0, users)
    def _(source):
        @pl.when((source >= dp) & (dp > 0))
        def _():
            line_copy(source, dp - 1, 0).wait_send()

        @pl.when((source <= dp) & (dp < users - 1))
        def _():
            line_copy(source, dp + 1, 1).wait_send()

    @pl.when(section > 0)
    def _():
        for c in range(chunks):
            pipe_copy(section - 1, c).wait_send()

    @pl.when(seq > 0)
    def _():
        for c in range(chunks):
            back_copy(seq - 1, c).wait_send()

    @pl.when(seq < shards - 1)
    def _():
        halo_copy(seq + 1).wait_send()


def on_device(
    section_input, event_ids, lengths, clicks, conversions, conv_weight, type_table, head_weight
):
    inputs_bf = section_input[0, 0]
    rows, width = inputs_bf.shape
    half = rows // 2
    kinds = type_table.shape[1]
    users, shards, sections = (lax.axis_size(name) for name in ("dp", "seq", "pipe"))
    group = users * shards
    share = KERNEL * width // group
    kind_share = kinds // group
    block_rows = share + -(-kind_share // 16) * 16
    vmem = pl.BlockSpec(memory_space=pltpu.VMEM)
    dma = pltpu.SemaphoreType.DMA
    f32, bf16 = jnp.float32, jnp.bfloat16
    conv, kind, grad_in = pl.pallas_call(
        functools.partial(kernel, users, shards, sections, kind_share),
        out_shape=(
            jax.ShapeDtypeStruct((share, width), f32),
            jax.ShapeDtypeStruct((kind_share, width), f32),
            jax.ShapeDtypeStruct((rows, width), bf16),
        ),
        in_specs=[
            vmem, vmem, vmem, vmem, pl.BlockSpec(memory_space=pltpu.SMEM),
            pl.BlockSpec(memory_space=pltpu.HBM), vmem, vmem,
        ],
        out_specs=(vmem, vmem, vmem),
        scratch_shapes=[
            pltpu.VMEM((KERNEL * width, width), bf16),
            pltpu.VMEM((rows + half, width), f32),
            pltpu.VMEM((KERNEL, rows, width), bf16),
            pltpu.VMEM((KERNEL - 1, rows, width), bf16),
            pltpu.VMEM((group, block_rows, rows), bf16),
            pltpu.VMEM((group, block_rows, rows), bf16),
            pltpu.VMEM((rows, width), f32),
            pltpu.VMEM((rows, width), f32),
            pltpu.VMEM((rows, width), f32),
            pltpu.VMEM((group * rows, width), bf16),
            pltpu.VMEM((half, width), bf16),
            pltpu.VMEM((half, width), bf16),
            pltpu.VMEM((half, width), bf16),
            pltpu.VMEM((rows, width), bf16),
            pltpu.VMEM((rows, width), bf16),
            pltpu.VMEM((8, width), f32),
            dma((KERNEL,)),
            dma((2,)),
            dma((2, width // BLOCK)),
            dma((2, width // BLOCK)),
            dma((group,)),
            dma((group,)),
            dma((users, 2)),
            dma((users,)),
            dma((users, shards)),
            dma((users, shards)),
        ],
        compiler_params=pltpu.CompilerParams(
            collective_id=0, has_side_effects=True, vmem_limit_bytes=58 * 1024 * 1024
        ),
    )(
        inputs_bf, event_ids, clicks, conversions, lengths, conv_weight[0], type_table[0],
        head_weight,
    )
    return (conv[None], kind[None], grad_in[None, None])


def solution(mesh):
    placed = (
        P("pipe", "dp", "seq", None),
        P("dp", "seq"),
        P("dp"),
        P("dp", "seq"),
        P("dp", "seq"),
        P("pipe", None, None),
        P("pipe", None, None),
        P(),
    )
    return jax.shard_map(
        on_device,
        mesh=mesh,
        in_specs=placed,
        out_specs=(
            P("pipe", ("dp", "seq"), None),
            P("pipe", ("dp", "seq"), None),
            P("pipe", "dp", "seq", None),
        ),
        check_vma=False,
    )
```
